32 devices in a mesh: fibre: 8 (over z, core), group: 4 (over y, x).
Axes of the slice: x: 2, y: 2, z: 4, core: 2. Of those that a mesh axis runs over, the one named last changes fastest.
Arguments:
- species_field: float32 [512, 32768], P('fibre', 'group'), may hold values from -45 to 45, as said below
- start_block: float32 [512, 64], replicated, may hold values from -4 to 4
Outputs:
- mode_basis: float32 [512, 64], replicated
- core_tensor: float32 [64, 32768], P(None, ('group', 'fibre'))
The draws below stay inside these ranges and needn't reach their ends.
Inputs may be any that keep to these rules, and one draw needn't show every extreme that they name: `species_field`: float32 field values.
All inputs are finite; a program needn't handle non-finite values.
Results may differ from the reference program's by a relative error of at most 0.0003.
Values sent between devices are 32-bit elements; how exact they have to be, the bound alone decides.
A program may use at most 64 MiB of HBM per device.

```python
import math
import jax
import jax.numpy as jnp
from jax import lax

I1 = 512
RANK = 64
ITERS = 3
COLS = 32768


def draw_species_field(key, part):
    keys = jax.random.split(key, 5)
    noise_draw = jax.random.truncated_normal(keys[0], -4.0, 4.0, (I1, COLS), jnp.float32)
    common_scale = 0.15
    upper_log = math.log(3.0)
    row_order = jax.random.permutation(keys[1], I1)
    mixed_noise = noise_draw + 0.6 * noise_draw[row_order]
    row_logs = jax.random.uniform(keys[2], (I1, 1), jnp.float32, 0.0, upper_log)
    position = jnp.arange(COLS, dtype=jnp.float32) / COLS
    amplitude = jnp.exp(row_logs * (2.0 * position[None, :] - 1.0)) * (0.6 + 1.2 * position[None, :])
    common_row = jax.random.truncated_normal(keys[3], -4.0, 4.0, (1, COLS), jnp.float32)
    common_weight = common_scale * jax.random.truncated_normal(keys[4], -4.0, 4.0, (I1, 1), jnp.float32)
    return (amplitude * mixed_noise + common_weight * common_row).astype(jnp.float32)


def noise(stream_key, shape, deviation, reach, kind=jnp.bfloat16):
    values = jax.random.normal(stream_key, shape, jnp.float32) * deviation
    return jnp.minimum(jnp.maximum(values, -reach), reach).astype(kind)


def setup_inputs(seed: int = 0) -> dict:
    key_of = jax.random.split(jax.random.key(seed), 3)
    species_field = draw_species_field(jax.random.fold_in(key_of[2], 71), 0)
    start_block = noise(key_of[1], (I1, RANK), 1.0, 4.0, jnp.float32)
    return dict(species_field=species_field, start_block=start_block)


highest_precision = lax.Precision.HIGHEST

def orthonormal(matrix):
    inner_gram = jnp.dot(matrix.T, matrix, precision=highest_precision)
    lower_factor = jnp.linalg.cholesky(inner_gram)
    return lax.linalg.triangular_solve(lower_factor, matrix, left_side=False, lower=True, transpose_a=True)

def reference(species_field, start_block):
    gram_matrix = jnp.dot(species_field, species_field.T, precision=highest_precision) / COLS
    mode_basis = orthonormal(start_block)
    for iteration in range(ITERS):
        mode_basis = orthonormal(jnp.dot(gram_matrix, mode_basis, precision=highest_precision))
    core_tensor = jnp.dot(mode_basis.T, species_field, precision=highest_precision)
    return (mode_basis, core_tensor)
```

```python
import functools

import jax
import jax.numpy as jnp
from jax import lax
from jax.experimental import pallas as pl
from jax.experimental.pallas import tpu as pltpu
from jax.sharding import PartitionSpec as P

ITERS = 3
TILE = 128
MESH = pl.DeviceIdType.MESH
HIGHEST = lax.Precision.HIGHEST


def contract(a, b, dims):
    return lax.dot_general(
        a, b, (dims, ((), ())), precision=HIGHEST, preferred_element_type=jnp.float32
    )


def aligned(start, size):
    return pl.ds(pl.multiple_of(start, 8), size)


def gram_kernel(
    nf, ng, scale, field, fib, out, part, r1, r2, r3, own_sem,
    a_send, a_recv, c_send, c_recv, g_send, g_recv, z_send, z_recv,
):
    f = lax.axis_index("fibre")
    g = lax.axis_index("group")
    nz = nf // 2
    core = lax.rem(f, 2)
    z = f // 2
    mate = f + 1 - 2 * core
    rows, width = field.shape[0], fib.shape[1]
    order = fib.shape[0]
    half = part.shape[0] // 2
    quarter = half // ng
    piece = quarter // nz

    def fibre_peer(o):
        return lax.rem(f + o, nf)

    def group_peer(o):
        return lax.rem(g + o, ng)

    def z_peer(o):
        return lax.rem(z + o, nz)

    barrier = pltpu.get_barrier_semaphore()
    for o in range(1, nf):
        pl.semaphore_signal(barrier, inc=1, device_id=(fibre_peer(o), g), device_id_type=MESH)
    for o in range(1, ng):
        pl.semaphore_signal(barrier, inc=1, device_id=(f, group_peer(o)), device_id_type=MESH)
    pl.semaphore_wait(barrier, nf + ng - 2)

    here = fib.at[aligned(f * rows, rows), :]
    sends = []
    for o in sorted(range(1, nf), key=lambda o: abs(o - nf // 2)):
        peer = fibre_peer(o)
        copy = pltpu.make_async_remote_copy(
            src_ref=field.at[:, pl.ds(pl.multiple_of(peer * width, TILE), width)],
            dst_ref=here,
            send_sem=a_send.at[o],
            recv_sem=a_recv.at[o],
            device_id=(peer, g),
            device_id_type=MESH,
        )
        copy.start()
        sends.append(copy)
    own = pltpu.make_async_copy(
        field.at[:, pl.ds(pl.multiple_of(f * width, TILE), width)], here, own_sem
    )
    own.start()
    own.wait()
    for copy in sends:
        copy.wait()

    blocks = order // TILE
    base = 0
    for pair in range(0, blocks, 2):
        top = min(pair + 2, blocks)
        strip = contract(fib[pair * TILE:top * TILE, :], fib[:top * TILE, :], ((1,), (1,)))
        for i in range(pair, top):
            for j in range(i + 1):
                part[base:base + TILE, :] = strip[(i - pair) * TILE:(i - pair + 1) * TILE, j * TILE:(j + 1) * TILE]
                base += TILE
    if base < part.shape[0]:
        part[base:, :] = jnp.zeros((part.shape[0] - base, TILE), jnp.float32)

    copy = pltpu.make_async_remote_copy(
        src_ref=part.at[aligned((1 - core) * half, half), :], dst_ref=r1,
        send_sem=c_send.at[0], recv_sem=c_recv.at[0], device_id=(mate, g), device_id_type=MESH,
    )
    copy.start()
    copy.wait()
    mine = core * half
    part[aligned(mine, half), :] += r1[...]

    sends = []
    for o in range(1, ng):
        peer = group_peer(o)
        copy = pltpu.make_async_remote_copy(
            src_ref=part.at[aligned(mine + peer * quarter, quarter), :], dst_ref=r2.at[o],
            send_sem=g_send.at[o], recv_sem=g_recv.at[o], device_id=(f, peer), device_id_type=MESH,
        )
        copy.start()
        sends.append(copy)
    for copy in sends:
        copy.wait()
    mine = mine + g * quarter
    total = part[aligned(mine, quarter), :]
    for o in range(1, ng):
        total += r2[o]
    part[aligned(mine, quarter), :] = total

    sends = []
    for o in range(1, nz):
        peer = z_peer(o)
        copy = pltpu.make_async_remote_copy(
            src_ref=part.at[aligned(mine + peer * piece, piece), :], dst_ref=r3.at[o],
            send_sem=z_send.at[o], recv_sem=z_recv.at[o],
            device_id=(peer * 2 + core, g), device_id_type=MESH,
        )
        copy.start()
        sends.append(copy)
    for copy in sends:
        copy.wait()
    last = mine + z * piece
    total = part[aligned(last, piece), :]
    for o in range(1, nz):
        total += r3[o]
    out[aligned(last, piece), :] = total * scale

    block = out.at[aligned(last, piece), :]
    sends = []
    for o in range(1, nz):
        copy = pltpu.make_async_remote_copy(
            src_ref=block, dst_ref=block, send_sem=z_send.at[nz + o], recv_sem=z_recv.at[nz + o],
            device_id=(z_peer(o) * 2 + core, g), device_id_type=MESH,
        )
        copy.start()
        sends.append(copy)
    for copy in sends:
        copy.wait()
    block = out.at[aligned(mine, quarter), :]
    sends = []
    for o in range(1, ng):
        copy = pltpu.make_async_remote_copy(
            src_ref=block, dst_ref=block, send_sem=g_send.at[ng + o], recv_sem=g_recv.at[ng + o],
            device_id=(f, group_peer(o)), device_id_type=MESH,
        )
        copy.start()
        sends.append(copy)
    for copy in sends:
        copy.wait()
    block = out.at[aligned(core * half, half), :]
    copy = pltpu.make_async_remote_copy(
        src_ref=block, dst_ref=block, send_sem=c_send.at[1], recv_sem=c_recv.at[1],
        device_id=(mate, g), device_id_type=MESH,
    )
    copy.start()
    copy.wait()


def inverse_factor(a, rows_ref):
    n = a.shape[0]
    eye = (
        lax.broadcasted_iota(jnp.int32, (n, n), 0) == lax.broadcasted_iota(jnp.int32, (n, n), 1)
    ).astype(jnp.float32)
    w = jnp.concatenate([a, eye], axis=1)
    for k in range(0, n, 8):
        left = n - k
        cols = [jnp.broadcast_to(w[:, k + j:k + j + 1], (left, 2 * n)) for j in range(8)]
        for j in range(8):
            pivot = cols[j][j:j + 1, :]
            inv = lax.rsqrt(pivot)
            inv = inv * (1.5 - 0.5 * pivot * inv * inv)
            row = w[j:j + 1, :] * inv
            rows_ref[k + j:k + j + 1, :] = row
            below = cols[j] * inv
            w = w - below * row
            for m in range(j + 1, 8):
                cols[m] = cols[m] - below * (cols[m][j:j + 1, :] * inv)
        w = w[8:, :]
    return rows_ref[:, n:]


def basis_kernel(packed, fib, start, basis, core, gram, held, rows_ref):
    order = fib.shape[0]
    blocks = order // TILE
    base = 0
    for i in range(blocks):
        for j in range(i + 1):
            block = packed[base:base + TILE, :]
            gram[i * TILE:(i + 1) * TILE, j * TILE:(j + 1) * TILE] = block
            if j < i:
                gram[j * TILE:(j + 1) * TILE, i * TILE:(i + 1) * TILE] = block.T
            base += TILE
    held[...] = start[...]

    def orth(step, carry):
        matrix = held[...]
        inverse = inverse_factor(contract(matrix, matrix, ((0,), (0,))), rows_ref)
        q = contract(matrix, inverse, ((1,), (1,)))
        basis[...] = q

        @pl.when(step < ITERS)
        def _():
            held[...] = contract(gram[...], q, ((1,), (0,)))

        return carry

    lax.fori_loop(0, ITERS + 1, orth, 0)
    core[...] = contract(basis[...], fib[...], ((0,), (0,)))


def on_device(nf, ng, field, start):
    rows, columns = field.shape
    order, rank = start.shape
    width = columns // nf
    blocks = order // TILE
    step = 8 * nf * ng
    packed_rows = -(-(blocks * (blocks + 1) // 2 * TILE) // step) * step
    half = packed_rows // 2
    quarter = half // ng
    piece = quarter // (nf // 2)
    vmem = pl.BlockSpec(memory_space=pltpu.VMEM)
    f32 = jnp.float32
    dma = pltpu.SemaphoreType.DMA
    fib, packed = pl.pallas_call(
        functools.partial(gram_kernel, nf, ng, 1.0 / (columns * ng)),
        out_shape=(
            jax.ShapeDtypeStruct((order, width), f32),
            jax.ShapeDtypeStruct((packed_rows, TILE), f32),
        ),
        in_specs=[vmem],
        out_specs=(vmem, vmem),
        scratch_shapes=[
            pltpu.VMEM((packed_rows, TILE), f32),
            pltpu.VMEM((half, TILE), f32),
            pltpu.VMEM((ng, quarter, TILE), f32),
            pltpu.VMEM((nf // 2, piece, TILE), f32),
            dma,
            dma((nf,)), dma((nf,)),
            dma((2,)), dma((2,)),
            dma((2 * ng,)), dma((2 * ng,)),
            dma((nf,)), dma((nf,)),
        ],
        compiler_params=pltpu.CompilerParams(
            collective_id=0, has_side_effects=True, vmem_limit_bytes=48 * 2**20
        ),
        name="gram",
    )(field)
    return pl.pallas_call(
        basis_kernel,
        out_shape=(
            jax.ShapeDtypeStruct((order, rank), f32),
            jax.ShapeDtypeStruct((rank, width), f32),
        ),
        in_specs=[vmem] * 3,
        out_specs=(vmem, vmem),
        scratch_shapes=[
            pltpu.VMEM((order, order), f32),
            pltpu.VMEM((order, rank), f32),
            pltpu.VMEM((rank, 2 * rank), f32),
        ],
        compiler_params=pltpu.CompilerParams(vmem_limit_bytes=48 * 2**20),
        name="basis",
    )(packed, fib, start)


def solution(mesh):
    nf, ng = mesh.shape["fibre"], mesh.shape["group"]
    return jax.shard_map(
        functools.partial(on_device, nf, ng),
        mesh=mesh,
        in_specs=(P("fibre", "group"), P()),
        out_specs=(P(), P(None, ("group", "fibre"))),
        check_vma=False,
    )
```

```python
import functools

import jax
import jax.numpy as jnp
from jax import lax
from jax.experimental import pallas as pl
from jax.experimental.pallas import tpu as pltpu
from jax.sharding import PartitionSpec as P

ITERS = 3
TILE = 128
MESH = pl.DeviceIdType.MESH
HIGHEST = lax.Precision.HIGHEST


def contract(a, b, dims):
    return lax.dot_general(
        a, b, (dims, ((), ())), precision=HIGHEST, preferred_element_type=jnp.float32
    )


def aligned(start, size):
    return pl.ds(pl.multiple_of(start, 8), size)


def inverse_factor(a, rows_ref):
    n = a.shape[0]
    eye = (
        lax.broadcasted_iota(jnp.int32, (n, n), 0) == lax.broadcasted_iota(jnp.int32, (n, n), 1)
    ).astype(jnp.float32)
    w = jnp.concatenate([a, eye], axis=1)
    for k in range(0, n, 8):
        left = n - k
        cols = [jnp.broadcast_to(w[:, k + j:k + j + 1], (left, 2 * n)) for j in range(8)]
        for j in range(8):
            pivot = cols[j][j:j + 1, :]
            inv = lax.rsqrt(pivot)
            inv = inv * (1.5 - 0.5 * pivot * inv * inv)
            row = w[j:j + 1, :] * inv
            rows_ref[k + j:k + j + 1, :] = row
            below = cols[j] * inv
            w = w - below * row
            for m in range(j + 1, 8):
                cols[m] = cols[m] - below * (cols[m][j:j + 1, :] * inv)
        w = w[8:, :]
    return rows_ref[:, n:]


def kernel(
    nf, ng, chunks, parts, scale, field, start, basis, core_out,
    fib, part, out, r1, r2, r3, gram, held, rows_ref, own_sem,
    a_send, a_recv, c_send, c_recv, g_send, g_recv, z_send, z_recv,
):
    f = lax.axis_index("fibre")
    g = lax.axis_index("group")
    nz = nf // 2
    core = lax.rem(f, 2)
    z = f // 2
    mate = f + 1 - 2 * core
    rows, width = field.shape[0], fib.shape[1]
    order = fib.shape[0]
    span = width // chunks

    def remote(src, dst, send, recv, slot, device):
        copy = pltpu.make_async_remote_copy(
            src_ref=src, dst_ref=dst, send_sem=send.at[slot], recv_sem=recv.at[slot],
            device_id=device, device_id_type=MESH,
        )
        copy.start()
        return copy

    def fibre_peer(o):
        return lax.rem(f + o, nf)

    def group_device(o):
        return (f, lax.rem(g + o, ng))

    def z_device(o):
        return (lax.rem(z + o, nz) * 2 + core, g)

    barrier = pltpu.get_barrier_semaphore()
    for o in range(1, nf):
        pl.semaphore_signal(barrier, inc=1, device_id=(fibre_peer(o), g), device_id_type=MESH)
    for o in range(1, ng):
        pl.semaphore_signal(barrier, inc=1, device_id=group_device(o), device_id_type=MESH)
    pl.semaphore_wait(barrier, nf + ng - 2)

    far_first = sorted(range(1, nf), key=lambda o: abs(o - nf // 2))
    sends = []
    owns = []
    for c in range(chunks):
        here = fib.at[aligned(f * rows, rows), c * span:(c + 1) * span]
        sends.append([
            remote(
                field.at[:, pl.ds(pl.multiple_of(fibre_peer(o) * width + c * span, TILE), span)],
                here, a_send, a_recv, c * nf + o, (fibre_peer(o), g),
            )
            for o in far_first
        ])
        own = pltpu.make_async_copy(
            field.at[:, pl.ds(pl.multiple_of(f * width + c * span, TILE), span)], here, own_sem.at[c]
        )
        own.start()
        owns.append(own)

    def orth(matrix):
        inverse = inverse_factor(contract(matrix, matrix, ((1,), (1,))), rows_ref)
        return contract(inverse, matrix, ((1,), (0,)))

    held[...] = orth(start[...])

    def summed(p, first, size):
        half = size // 2
        quarter = half // ng
        piece = quarter // nz
        mine = first + core * half
        other = first + (1 - core) * half
        copy = remote(part.at[aligned(other, half), :], r1.at[0:half, :] if p == 0 else r1.at[r1.shape[0] - half:, :],
                      c_send, c_recv, 2 * p, (mate, g))
        yield
        copy.wait()
        base1 = 0 if p == 0 else r1.shape[0] - half
        part[aligned(mine, half), :] += r1[base1:base1 + half, :]

        at2 = 0 if p == 0 else r2.shape[1] - quarter
        copies = [
            remote(part.at[aligned(mine + lax.rem(g + o, ng) * quarter, quarter), :],
                   r2.at[o, at2:at2 + quarter, :], g_send, g_recv, 2 * p * ng + o, group_device(o))
            for o in range(1, ng)
        ]
        yield
        for copy in copies:
            copy.wait()
        mine = mine + g * quarter
        total = part[aligned(mine, quarter), :]
        for o in range(1, ng):
            total += r2[o, at2:at2 + quarter, :]
        part[aligned(mine, quarter), :] = total

        at3 = 0 if p == 0 else r3.shape[1] - piece
        copies = [
            remote(part.at[aligned(mine + lax.rem(z + o, nz) * piece, piece), :],
                   r3.at[o, at3:at3 + piece, :], z_send, z_recv, 2 * p * nz + o, z_device(o))
            for o in range(1, nz)
        ]
        yield
        for copy in copies:
            copy.wait()
        last = mine + z * piece
        total = part[aligned(last, piece), :]
        for o in range(1, nz):
            total += r3[o, at3:at3 + piece, :]
        out[aligned(last, piece), :] = total * scale

        block = out.at[aligned(last, piece), :]
        copies = [
            remote(block, block, z_send, z_recv, (2 * p + 1) * nz + o, z_device(o))
            for o in range(1, nz)
        ]
        yield
        for copy in copies:
            copy.wait()
        block = out.at[aligned(mine, quarter), :]
        copies = [
            remote(block, block, g_send, g_recv, (2 * p + 1) * ng + o, group_device(o))
            for o in range(1, ng)
        ]
        yield
        for copy in copies:
            copy.wait()
        block = out.at[aligned(first + core * half, half), :]
        copy = remote(block, block, c_send, c_recv, 2 * p + 1, (mate, g))
        yield
        copy.wait()

    blocks = order // TILE
    places = {}
    for pair in reversed(range(0, blocks, 2)):
        for i in range(pair, min(pair + 2, blocks)):
            for j in range(i + 1):
                places[i, j] = len(places) * TILE
    filled = len(places) * TILE
    if filled < part.shape[0]:
        part[filled:, :] = jnp.zeros((part.shape[0] - filled, TILE), jnp.float32)
    sums = []
    for c in range(chunks):
        for copy in sends[c]:
            copy.wait_recv()
        owns[c].wait()
        columns = slice(c * span, (c + 1) * span)
        done = 0
        for pair in reversed(range(0, blocks, 2)):
            top = min(pair + 2, blocks)
            strip = contract(fib[pair * TILE:top * TILE, columns], fib[:top * TILE, columns], ((1,), (1,)))
            for i in range(pair, top):
                for j in range(i + 1):
                    block = strip[(i - pair) * TILE:(i - pair + 1) * TILE, j * TILE:(j + 1) * TILE]
                    at = slice(places[i, j], places[i, j] + TILE)
                    part[at, :] = block if c == 0 else part[at, :] + block
                    done += TILE
            if c == chunks - 1:
                ready = part.shape[0] if done == filled else done
                while len(sums) < len(parts) and sum(parts[len(sums)]) <= ready:
                    step = summed(len(sums), *parts[len(sums)])
                    next(step)
                    sums.append(step)
    going = list(sums)
    while going:
        for step in list(going):
            try:
                next(step)
            except StopIteration:
                going.remove(step)

    for (i, j), at in places.items():
        block = out[at:at + TILE, :]
        gram[i * TILE:(i + 1) * TILE, j * TILE:(j + 1) * TILE] = block
        if j < i:
            gram[j * TILE:(j + 1) * TILE, i * TILE:(i + 1) * TILE] = block.T

    def iterate(step, carry):
        held[...] = orth(contract(held[...], gram[...], ((1,), (0,))))
        return carry

    lax.fori_loop(0, ITERS, iterate, 0)
    basis[...] = held[...]
    core_out[...] = contract(held[...], fib[...], ((1,), (0,)))
    for copies in sends:
        for copy in copies:
            copy.wait_send()


def on_device(nf, ng, field, start):
    rows, columns = field.shape
    order, rank = start.shape
    width = columns // nf
    chunks = 4
    blocks = order // TILE
    unit = 8 * nf * ng
    units = -(-(blocks * (blocks + 1) // 2 * TILE) // unit)
    sizes = [n * unit for n in (units - units // 2, units // 2) if n]
    parts = [(sum(sizes[:p]), size) for p, size in enumerate(sizes)]
    packed_rows = sum(sizes)
    vmem = pl.BlockSpec(memory_space=pltpu.VMEM)
    f32 = jnp.float32
    dma = pltpu.SemaphoreType.DMA
    basis, core = pl.pallas_call(
        functools.partial(kernel, nf, ng, chunks, parts, 1.0 / (columns * ng)),
        out_shape=(
            jax.ShapeDtypeStruct((rank, order), f32),
            jax.ShapeDtypeStruct((rank, width), f32),
        ),
        in_specs=[pl.BlockSpec(memory_space=pl.ANY), vmem],
        out_specs=(vmem, vmem),
        scratch_shapes=[
            pltpu.VMEM((order, width), f32),
            pltpu.VMEM((packed_rows, TILE), f32),
            pltpu.VMEM((packed_rows, TILE), f32),
            pltpu.VMEM((packed_rows // 2, TILE), f32),
            pltpu.VMEM((ng, packed_rows // 2 // ng, TILE), f32),
            pltpu.VMEM((nf // 2, packed_rows // nf // ng, TILE), f32),
            pltpu.VMEM((order, order), f32),
            pltpu.VMEM((rank, order), f32),
            pltpu.VMEM((rank, 2 * rank), f32),
            dma((chunks,)),
            dma((chunks * nf,)), dma((chunks * nf,)),
            dma((4,)), dma((4,)),
            dma((4 * ng,)), dma((4 * ng,)),
            dma((2 * nf,)), dma((2 * nf,)),
        ],
        compiler_params=pltpu.CompilerParams(
            collective_id=0, has_side_effects=True, vmem_limit_bytes=56 * 2**20
        ),
        name="subspace",
    )(field, start.T)
    return basis.T, core


def solution(mesh):
    nf, ng = mesh.shape["fibre"], mesh.shape["group"]
    return jax.shard_map(
        functools.partial(on_device, nf, ng),
        mesh=mesh,
        in_specs=(P("fibre", "group"), P()),
        out_specs=(P(), P(None, ("group", "fibre"))),
        check_vma=False,
    )
```

```python
import functools

import jax
import jax.numpy as jnp
from jax import lax
from jax.experimental import pallas as pl
from jax.experimental.pallas import tpu as pltpu
from jax.sharding import PartitionSpec as P

ITERS = 3
TILE = 128
MESH = pl.DeviceIdType.MESH
HIGHEST = lax.Precision.HIGHEST


def contract(a, b, dims):
    return lax.dot_general(
        a, b, (dims, ((), ())), precision=HIGHEST, preferred_element_type=jnp.float32
    )


def aligned(start, size):
    return pl.ds(pl.multiple_of(start, 8), size)


def inverse_factor(a, rows_ref):
    n = a.shape[0]
    eye = (
        lax.broadcasted_iota(jnp.int32, (n, n), 0) == lax.broadcasted_iota(jnp.int32, (n, n), 1)
    ).astype(jnp.float32)
    w = jnp.concatenate([a, eye], axis=1)
    for k in range(0, n, 8):
        left = n - k
        cols = [jnp.broadcast_to(w[:, k + j:k + j + 1], (left, 2 * n)) for j in range(8)]
        for j in range(8):
            pivot = cols[j][j:j + 1, :]
            inv = lax.rsqrt(pivot)
            inv = inv * (1.5 - 0.5 * pivot * inv * inv)
            row = w[j:j + 1, :] * inv
            rows_ref[k + j:k + j + 1, :] = row
            below = cols[j] * inv
            w = w - below * row
            for m in range(j + 1, 8):
                cols[m] = cols[m] - below * (cols[m][j:j + 1, :] * inv)
        w = w[8:, :]
    return rows_ref[:, n:]


def row_order(rows, first, count):
    n = rows * count
    assert rows & (rows - 1) == 0
    at = lax.broadcasted_iota(jnp.int32, (n, n), 0)
    source = lax.shift_right_logical(at, rows.bit_length() - 1)
    r = at & (rows - 1)
    place = jnp.where(r < first, source * first + r, count * first + source * (rows - first) + r - first)
    return (place == lax.broadcasted_iota(jnp.int32, (n, n), 1)).astype(jnp.float32)


def orth(matrix, rows_ref):
    inverse = inverse_factor(contract(matrix, matrix, ((1,), (1,))), rows_ref)
    return contract(inverse, matrix, ((1,), (0,)))


def gram_kernel(
    nf, ng, first, sizes, scale, field, start, fib, out, held,
    part, r1, r2, r3, rows_ref, own_sem,
    a_send, a_recv, c_send, c_recv, z_send, z_recv,
):
    f = lax.axis_index("fibre")
    g = lax.axis_index("group")
    nz = nf // 2
    plane = 2 * ng
    core = lax.rem(f, 2)
    z = f // 2
    u = g * 2 + core
    rows, width = field.shape[0], fib.shape[1]

    def remote(src, dst, send, recv, slot, device):
        copy = pltpu.make_async_remote_copy(
            src_ref=src, dst_ref=dst, send_sem=send.at[slot], recv_sem=recv.at[slot],
            device_id=device, device_id_type=MESH,
        )
        copy.start()
        return copy

    def fibre_peer(o):
        return lax.rem(f + o, nf)

    def plane_peer(o):
        return lax.rem(u + o, plane)

    def plane_device(o):
        v = plane_peer(o)
        return (z * 2 + lax.rem(v, 2), v // 2)

    def z_device(o):
        return (lax.rem(z + o, nz) * 2 + core, g)

    barrier = pltpu.get_barrier_semaphore()
    for o in range(1, nf):
        pl.semaphore_signal(barrier, inc=1, device_id=(fibre_peer(o), g), device_id_type=MESH)
    for o in range(1, plane):
        pl.semaphore_signal(barrier, inc=1, device_id=plane_device(o), device_id_type=MESH)
    pl.semaphore_wait(barrier, nf + plane - 2)

    far_first = sorted(range(1, nf), key=lambda o: abs(o - nf // 2))
    bounds = ((0, first), (first, rows))
    sends, owns = [], []
    for c, (low, high) in enumerate(bounds):
        here = fib.at[aligned(nf * low + f * (high - low), high - low), :]
        sends.append([
            remote(
                field.at[low:high, pl.ds(pl.multiple_of(fibre_peer(o) * width, TILE), width)],
                here, a_send, a_recv, c * nf + o, (fibre_peer(o), g),
            )
            for o in far_first
        ])
        own = pltpu.make_async_copy(
            field.at[low:high, pl.ds(pl.multiple_of(f * width, TILE), width)], here, own_sem.at[c]
        )
        own.start()
        owns.append(own)

    held[...] = orth(contract(start[...], row_order(rows, first, nf), ((1,), (0,))), rows_ref)

    def summed(p):
        begin, size = sum(sizes[:p]), sizes[p]
        eighth = size // plane
        piece = eighth // nz
        at1 = 0 if p == 0 else r1.shape[1] - eighth
        at2 = 0 if p == 0 else r2.shape[1] - piece
        copies = [
            remote(part.at[aligned(begin + plane_peer(o) * eighth, eighth), :],
                   r1.at[o, at1:at1 + eighth, :], c_send, c_recv, 2 * p * plane + o, plane_device(o))
            for o in range(1, plane)
        ]
        yield
        for copy in copies:
            copy.wait()
        mine = begin + u * eighth
        total = part[aligned(mine, eighth), :]
        for o in range(1, plane):
            total += r1[o, at1:at1 + eighth, :]

        if p == 0:
            part[aligned(mine, eighth), :] = total
            copies = [
                remote(part.at[aligned(mine + lax.rem(z + o, nz) * piece, piece), :],
                       r2.at[o, at2:at2 + piece, :], z_send, z_recv, o, z_device(o))
                for o in range(1, nz)
            ]
            yield
            for copy in copies:
                copy.wait()
            last = mine + z * piece
            total = part[aligned(last, piece), :]
            for o in range(1, nz):
                total += r2[o, at2:at2 + piece, :]
            out[aligned(last, piece), :] = total * scale
            block = out.at[aligned(last, piece), :]
            copies = [
                remote(block, block, z_send, z_recv, nz + o, z_device(o)) for o in range(1, nz)
            ]
            yield
            for copy in copies:
                copy.wait()
        else:
            r3[z] = total
            copies = [
                remote(r3.at[z], r3.at[z], z_send, z_recv, 2 * nz + o, z_device(o))
                for o in range(1, nz)
            ]
            yield
            for copy in copies:
                copy.wait()
            total = r3[0]
            for n in range(1, nz):
                total += r3[n]
            out[aligned(mine, eighth), :] = total * scale

        block = out.at[aligned(mine, eighth), :]
        copies = [
            remote(block, block, c_send, c_recv, (2 * p + 1) * plane + o, plane_device(o))
            for o in range(1, plane)
        ]
        yield
        for copy in copies:
            copy.wait()

    going = []
    for c, (low, high) in enumerate(bounds):
        for copy in sends[c]:
            copy.wait_recv()
        owns[c].wait()
        begin = sum(sizes[:c])
        base = begin
        end = nf * high // TILE
        for pair in range(nf * low // TILE, end, 2):
            top = min(pair + 2, end)
            strip = contract(fib[pair * TILE:top * TILE, :], fib[:top * TILE, :], ((1,), (1,)))
            for i in range(pair, top):
                for j in range(i + 1):
                    part[base:base + TILE, :] = strip[(i - pair) * TILE:(i - pair + 1) * TILE, j * TILE:(j + 1) * TILE]
                    base += TILE
        if base < begin + sizes[c]:
            part[base:begin + sizes[c], :] = jnp.zeros((begin + sizes[c] - base, TILE), jnp.float32)
        step = summed(c)
        next(step)
        going.append(step)
        if c == 0:
            next(step)
    going.reverse()
    while going:
        for step in list(going):
            try:
                next(step)
            except StopIteration:
                going.remove(step)
    for copies in sends:
        for copy in copies:
            copy.wait_send()


def basis_kernel(nf, first, sizes, packed, fib, begin, basis, core, gram, held, rows_ref):
    order = fib.shape[0]
    split = nf * first // TILE
    base = 0
    for i in range(order // TILE):
        if i == split:
            base = sizes[0]
        for j in range(i + 1):
            block = packed[base:base + TILE, :]
            gram[i * TILE:(i + 1) * TILE, j * TILE:(j + 1) * TILE] = block
            if j < i:
                gram[j * TILE:(j + 1) * TILE, i * TILE:(i + 1) * TILE] = block.T
            base += TILE
    held[...] = begin[...]

    def iterate(step, carry):
        held[...] = orth(contract(held[...], gram[...], ((1,), (0,))), rows_ref)
        return carry

    lax.fori_loop(0, ITERS, iterate, 0)
    basis[...] = contract(held[...], row_order(order // nf, first, nf), ((1,), (1,)))
    core[...] = contract(held[...], fib[...], ((1,), (0,)))


def on_device(nf, ng, field, start):
    rows, columns = field.shape
    order, rank = start.shape
    width = columns // nf
    first = rows * 3 // 4 if rows % 32 == 0 else rows // 2
    blocks, early = order // TILE, nf * first // TILE
    unit = 8 * nf * ng
    counts = (early * (early + 1) // 2, blocks * (blocks + 1) // 2 - early * (early + 1) // 2)
    sizes = [-(-(n * TILE) // unit) * unit for n in counts]
    packed_rows = sum(sizes)
    plane, nz = 2 * ng, nf // 2
    vmem = pl.BlockSpec(memory_space=pltpu.VMEM)
    f32 = jnp.float32
    dma = pltpu.SemaphoreType.DMA
    fib, packed, begin = pl.pallas_call(
        functools.partial(gram_kernel, nf, ng, first, sizes, 1.0 / (columns * ng)),
        out_shape=(
            jax.ShapeDtypeStruct((order, width), f32),
            jax.ShapeDtypeStruct((packed_rows, TILE), f32),
            jax.ShapeDtypeStruct((rank, order), f32),
        ),
        in_specs=[pl.BlockSpec(memory_space=pl.ANY), vmem],
        out_specs=(vmem, vmem, vmem),
        scratch_shapes=[
            pltpu.VMEM((packed_rows, TILE), f32),
            pltpu.VMEM((plane, packed_rows // plane, TILE), f32),
            pltpu.VMEM((nz, sizes[0] // plane // nz, TILE), f32),
            pltpu.VMEM((nz, sizes[1] // plane, TILE), f32),
            pltpu.VMEM((rank, 2 * rank), f32),
            dma((2,)),
            dma((2 * nf,)), dma((2 * nf,)),
            dma((4 * plane,)), dma((4 * plane,)),
            dma((3 * nz,)), dma((3 * nz,)),
        ],
        compiler_params=pltpu.CompilerParams(
            collective_id=0, has_side_effects=True, vmem_limit_bytes=48 * 2**20
        ),
        name="gram",
    )(field, start.T)
    basis, core = pl.pallas_call(
        functools.partial(basis_kernel, nf, first, sizes),
        out_shape=(
            jax.ShapeDtypeStruct((rank, order), f32),
            jax.ShapeDtypeStruct((rank, width), f32),
        ),
        in_specs=[vmem] * 3,
        out_specs=(vmem, vmem),
        scratch_shapes=[
            pltpu.VMEM((order, order), f32),
            pltpu.VMEM((rank, order), f32),
            pltpu.VMEM((rank, 2 * rank), f32),
        ],
        compiler_params=pltpu.CompilerParams(vmem_limit_bytes=48 * 2**20),
        name="basis",
    )(packed, fib, begin)
    return basis.T, core


def solution(mesh):
    nf, ng = mesh.shape["fibre"], mesh.shape["group"]
    return jax.shard_map(
        functools.partial(on_device, nf, ng),
        mesh=mesh,
        in_specs=(P("fibre", "group"), P()),
        out_specs=(P(), P(None, ("group", "fibre"))),
        check_vma=False,
    )
```

```python
import functools

import jax
import jax.numpy as jnp
from jax import lax
from jax.experimental import pallas as pl
from jax.experimental.pallas import tpu as pltpu
from jax.sharding import PartitionSpec as P

ITERS = 3
TILE = 128
MESH = pl.DeviceIdType.MESH
HIGHEST = lax.Precision.HIGHEST


def contract(a, b, dims):
    return lax.dot_general(
        a, b, (dims, ((), ())), precision=HIGHEST, preferred_element_type=jnp.float32
    )


def aligned(start, size):
    return pl.ds(pl.multiple_of(start, 8), size)


def inverse_factor(a, rows_ref):
    n = a.shape[0]
    eye = (
        lax.broadcasted_iota(jnp.int32, (n, n), 0) == lax.broadcasted_iota(jnp.int32, (n, n), 1)
    ).astype(jnp.float32)
    w = jnp.concatenate([a, eye], axis=1)
    for k in range(0, n, 8):
        left = n - k
        cols = [jnp.broadcast_to(w[:, k + j:k + j + 1], (left, 2 * n)) for j in range(8)]
        for j in range(8):
            pivot = cols[j][j:j + 1, :]
            inv = lax.rsqrt(pivot)
            inv = inv * (1.5 - 0.5 * pivot * inv * inv)
            row = w[j:j + 1, :] * inv
            rows_ref[k + j:k + j + 1, :] = row
            below = cols[j] * inv
            w = w - below * row
            for m in range(j + 1, 8):
                cols[m] = cols[m] - below * (cols[m][j:j + 1, :] * inv)
        w = w[8:, :]
    return rows_ref[:, n:]


def row_order(rows, first, count):
    n = rows * count
    assert rows & (rows - 1) == 0
    at = lax.broadcasted_iota(jnp.int32, (n, n), 0)
    source = lax.shift_right_logical(at, rows.bit_length() - 1)
    r = at & (rows - 1)
    place = jnp.where(r < first, source * first + r, count * first + source * (rows - first) + r - first)
    return (place == lax.broadcasted_iota(jnp.int32, (n, n), 1)).astype(jnp.float32)


def orth(matrix, rows_ref):
    inverse = inverse_factor(contract(matrix, matrix, ((1,), (1,))), rows_ref)
    return contract(inverse, matrix, ((1,), (0,)))


def gram_kernel(
    nf, ng, first, sizes, scale, field, start, fib, out, held,
    part, r1, r2, r3, rows_ref, own_sem,
    a_send, a_recv, c_send, c_recv, z_send, z_recv,
):
    f = lax.axis_index("fibre")
    g = lax.axis_index("group")
    nz = nf // 2
    plane = 2 * ng
    core = lax.rem(f, 2)
    z = f // 2
    u = g * 2 + core
    rows, width = field.shape[0], fib.shape[1]

    def remote(src, dst, send, recv, slot, device, start=True):
        copy = pltpu.make_async_remote_copy(
            src_ref=src, dst_ref=dst, send_sem=send.at[slot], recv_sem=recv.at[slot],
            device_id=device, device_id_type=MESH,
        )
        if start:
            copy.start()
        return copy

    def fibre_peer(o):
        peer = f
        for bit in range(o.bit_length()):
            if o >> bit & 1:
                peer = peer + 2**bit - 2 * 2**bit * lax.rem(f // 2**bit, 2)
        return peer

    def plane_peer(o):
        return lax.rem(u + o, plane)

    def plane_device(o):
        v = plane_peer(o)
        return (z * 2 + lax.rem(v, 2), v // 2)

    def z_device(o):
        return (lax.rem(z + o, nz) * 2 + core, g)

    barrier = pltpu.get_barrier_semaphore()
    for o in range(1, nf):
        pl.semaphore_signal(barrier, inc=1, device_id=(fibre_peer(o), g), device_id_type=MESH)
    for o in range(1, plane):
        pl.semaphore_signal(barrier, inc=1, device_id=plane_device(o), device_id_type=MESH)
    pl.semaphore_wait(barrier, nf + plane - 2)

    assert nf & (nf - 1) == 0
    inner = lax.rem((z + 1) // 2, 2)
    near = [o for o in range(2, nf) if o < 4]
    far = [o for o in range(2, nf) if o >= 4]
    bounds = ((0, first), (first, rows))
    sends, owns = [], []
    for c, (low, high) in enumerate(bounds):
        here = fib.at[aligned(nf * low + f * (high - low), high - low), :]
        copies = {
            o: remote(
                field.at[low:high, pl.ds(pl.multiple_of(fibre_peer(o) * width, TILE), width)],
                here, a_send, a_recv, c * nf + o, (fibre_peer(o), g), start=False,
            )
            for o in range(1, nf)
        }

        @pl.when(inner == 0)
        def _():
            for o in near + far + [1]:
                copies[o].start()

        @pl.when(inner == 1)
        def _():
            for o in far + near + [1]:
                copies[o].start()

        sends.append(list(copies.values()))
        own = pltpu.make_async_copy(
            field.at[low:high, pl.ds(pl.multiple_of(f * width, TILE), width)], here, own_sem.at[c]
        )
        own.start()
        owns.append(own)

    begin = pltpu.make_async_copy(start, held, own_sem.at[2])
    begin.start()
    begin.wait()
    held[...] = orth(contract(held[...], row_order(rows, first, nf), ((1,), (0,))), rows_ref)

    def summed(p):
        begin, size = sum(sizes[:p]), sizes[p]
        eighth = size // plane
        piece = eighth // nz
        at1 = 0 if p == 0 else r1.shape[1] - eighth
        at2 = 0 if p == 0 else r2.shape[1] - piece
        copies = [
            remote(part.at[aligned(begin + plane_peer(o) * eighth, eighth), :],
                   r1.at[o, at1:at1 + eighth, :], c_send, c_recv, 2 * p * plane + o, plane_device(o))
            for o in range(1, plane)
        ]
        yield
        for copy in copies:
            copy.wait()
        mine = begin + u * eighth
        total = part[aligned(mine, eighth), :]
        for o in range(1, plane):
            total += r1[o, at1:at1 + eighth, :]

        if p == 0:
            part[aligned(mine, eighth), :] = total
            copies = [
                remote(part.at[aligned(mine + lax.rem(z + o, nz) * piece, piece), :],
                       r2.at[o, at2:at2 + piece, :], z_send, z_recv, o, z_device(o))
                for o in range(1, nz)
            ]
            yield
            for copy in copies:
                copy.wait()
            last = mine + z * piece
            total = part[aligned(last, piece), :]
            for o in range(1, nz):
                total += r2[o, at2:at2 + piece, :]
            out[aligned(last, piece), :] = total * scale
            block = out.at[aligned(last, piece), :]
            copies = [
                remote(block, block, z_send, z_recv, nz + o, z_device(o)) for o in range(1, nz)
            ]
            yield
            for copy in copies:
                copy.wait()
        else:
            r3[z] = total
            copies = [
                remote(r3.at[z], r3.at[z], z_send, z_recv, 2 * nz + o, z_device(o))
                for o in range(1, nz)
            ]
            yield
            for copy in copies:
                copy.wait()
            total = r3[0]
            for n in range(1, nz):
                total += r3[n]
            out[aligned(mine, eighth), :] = total * scale

        block = out.at[aligned(mine, eighth), :]
        copies = [
            remote(block, block, c_send, c_recv, (2 * p + 1) * plane + o, plane_device(o))
            for o in range(1, plane)
        ]
        yield
        for copy in copies:
            copy.wait()

    going = []
    for c, (low, high) in enumerate(bounds):
        for copy in sends[c]:
            copy.wait_recv()
        owns[c].wait()
        begin = sum(sizes[:c])
        base = begin
        end = nf * high // TILE
        for pair in range(nf * low // TILE, end, 2):
            top = min(pair + 2, end)
            strip = contract(fib[pair * TILE:top * TILE, :], fib[:top * TILE, :], ((1,), (1,)))
            for i in range(pair, top):
                for j in range(i + 1):
                    part[base:base + TILE, :] = strip[(i - pair) * TILE:(i - pair + 1) * TILE, j * TILE:(j + 1) * TILE]
                    base += TILE
        if base < begin + sizes[c]:
            part[base:begin + sizes[c], :] = jnp.zeros((begin + sizes[c] - base, TILE), jnp.float32)
        step = summed(c)
        next(step)
        going.append(step)
    going.reverse()
    while going:
        for step in list(going):
            try:
                next(step)
            except StopIteration:
                going.remove(step)
    for copies in sends:
        for copy in copies:
            copy.wait_send()


def basis_kernel(nf, first, sizes, packed, fib, begin, basis, core, gram, held, rows_ref):
    order = fib.shape[0]
    split = nf * first // TILE
    base = 0
    for i in range(order // TILE):
        if i == split:
            base = sizes[0]
        for j in range(i + 1):
            block = packed[base:base + TILE, :]
            gram[i * TILE:(i + 1) * TILE, j * TILE:(j + 1) * TILE] = block
            if j < i:
                gram[j * TILE:(j + 1) * TILE, i * TILE:(i + 1) * TILE] = block.T
            base += TILE
    held[...] = begin[...]

    def iterate(step, carry):
        held[...] = orth(contract(held[...], gram[...], ((1,), (0,))), rows_ref)
        return carry

    lax.fori_loop(0, ITERS, iterate, 0)
    basis[...] = contract(held[...], row_order(order // nf, first, nf), ((1,), (1,)))
    core[...] = contract(held[...], fib[...], ((1,), (0,)))


def on_device(nf, ng, field, start):
    rows, columns = field.shape
    order, rank = start.shape
    width = columns // nf
    first = rows * 3 // 4 if rows % 32 == 0 else rows // 2
    blocks, early = order // TILE, nf * first // TILE
    unit = 8 * nf * ng
    counts = (early * (early + 1) // 2, blocks * (blocks + 1) // 2 - early * (early + 1) // 2)
    sizes = [-(-(n * TILE) // unit) * unit for n in counts]
    packed_rows = sum(sizes)
    plane, nz = 2 * ng, nf // 2
    vmem = pl.BlockSpec(memory_space=pltpu.VMEM)
    f32 = jnp.float32
    dma = pltpu.SemaphoreType.DMA
    fib, packed, begin = pl.pallas_call(
        functools.partial(gram_kernel, nf, ng, first, sizes, 1.0 / (columns * ng)),
        out_shape=(
            jax.ShapeDtypeStruct((order, width), f32),
            jax.ShapeDtypeStruct((packed_rows, TILE), f32),
            jax.ShapeDtypeStruct((rank, order), f32),
        ),
        in_specs=[pl.BlockSpec(memory_space=pltpu.HBM)] * 2,
        out_specs=(vmem, vmem, vmem),
        scratch_shapes=[
            pltpu.VMEM((packed_rows, TILE), f32),
            pltpu.VMEM((plane, packed_rows // plane, TILE), f32),
            pltpu.VMEM((nz, sizes[0] // plane // nz, TILE), f32),
            pltpu.VMEM((nz, sizes[1] // plane, TILE), f32),
            pltpu.VMEM((rank, 2 * rank), f32),
            dma((3,)),
            dma((2 * nf,)), dma((2 * nf,)),
            dma((4 * plane,)), dma((4 * plane,)),
            dma((3 * nz,)), dma((3 * nz,)),
        ],
        compiler_params=pltpu.CompilerParams(
            collective_id=0, has_side_effects=True, vmem_limit_bytes=48 * 2**20
        ),
        name="gram",
    )(field, start.T)
    basis, core = pl.pallas_call(
        functools.partial(basis_kernel, nf, first, sizes),
        out_shape=(
            jax.ShapeDtypeStruct((rank, order), f32),
            jax.ShapeDtypeStruct((rank, width), f32),
        ),
        in_specs=[vmem] * 3,
        out_specs=(vmem, vmem),
        scratch_shapes=[
            pltpu.VMEM((order, order), f32),
            pltpu.VMEM((rank, order), f32),
            pltpu.VMEM((rank, 2 * rank), f32),
        ],
        compiler_params=pltpu.CompilerParams(vmem_limit_bytes=48 * 2**20),
        name="basis",
    )(packed, fib, begin)
    return basis.T, core


def solution(mesh):
    nf, ng = mesh.shape["fibre"], mesh.shape["group"]
    return jax.shard_map(
        functools.partial(on_device, nf, ng),
        mesh=mesh,
        in_specs=(P("fibre", "group"), P()),
        out_specs=(P(), P(None, ("group", "fibre"))),
        check_vma=False,
    )
```

```python
import functools

import jax
import jax.numpy as jnp
from jax import lax
from jax.experimental import pallas as pl
from jax.experimental.pallas import tpu as pltpu
from jax.sharding import PartitionSpec as P

ITERS = 3
TILE = 128
MESH = pl.DeviceIdType.MESH
HIGHEST = lax.Precision.HIGHEST


def contract(a, b, dims):
    return lax.dot_general(
        a, b, (dims, ((), ())), precision=HIGHEST, preferred_element_type=jnp.float32
    )


def aligned(start, size):
    return pl.ds(pl.multiple_of(start, 8), size)


def inverse_factor(a, rows_ref):
    n = a.shape[0]
    eye = (
        lax.broadcasted_iota(jnp.int32, (n, n), 0) == lax.broadcasted_iota(jnp.int32, (n, n), 1)
    ).astype(jnp.float32)
    w = jnp.concatenate([a, eye], axis=1)
    for k in range(0, n, 8):
        left = n - k
        cols = [jnp.broadcast_to(w[:, k + j:k + j + 1], (left, 2 * n)) for j in range(8)]
        for j in range(8):
            pivot = cols[j][j:j + 1, :]
            inv = lax.rsqrt(pivot)
            inv = inv * (1.5 - 0.5 * pivot * inv * inv)
            row = w[j:j + 1, :] * inv
            rows_ref[k + j:k + j + 1, :] = row
            below = cols[j] * inv
            w = w - below * row
            for m in range(j + 1, 8):
                cols[m] = cols[m] - below * (cols[m][j:j + 1, :] * inv)
        w = w[8:, :]
    return rows_ref[:, n:]


def row_order(rows, first, count):
    n = rows * count
    assert rows & (rows - 1) == 0
    at = lax.broadcasted_iota(jnp.int32, (n, n), 0)
    source = lax.shift_right_logical(at, rows.bit_length() - 1)
    r = at & (rows - 1)
    place = jnp.where(r < first, source * first + r, count * first + source * (rows - first) + r - first)
    return (place == lax.broadcasted_iota(jnp.int32, (n, n), 1)).astype(jnp.float32)


def orth(matrix, rows_ref):
    inverse = inverse_factor(contract(matrix, matrix, ((1,), (1,))), rows_ref)
    return contract(inverse, matrix, ((1,), (0,)))


def gram_kernel(
    nf, ng, first, sizes, scale, field, start, fib, out, held,
    part, r1, r2, r3, rows_ref, own_sem,
    a_send, a_recv, c_send, c_recv, z_send, z_recv,
):
    f = lax.axis_index("fibre")
    g = lax.axis_index("group")
    nz = nf // 2
    plane = 2 * ng
    core = lax.rem(f, 2)
    z = f // 2
    u = g * 2 + core
    rows, width = field.shape[0], fib.shape[1]

    def remote(src, dst, send, recv, slot, device, start=True):
        copy = pltpu.make_async_remote_copy(
            src_ref=src, dst_ref=dst, send_sem=send.at[slot], recv_sem=recv.at[slot],
            device_id=device, device_id_type=MESH,
        )
        if start:
            copy.start()
        return copy

    def fibre_peer(o):
        peer = f
        for bit in range(o.bit_length()):
            if o >> bit & 1:
                peer = peer + 2**bit - 2 * 2**bit * lax.rem(f // 2**bit, 2)
        return peer

    def plane_peer(o):
        return lax.rem(u + o, plane)

    def plane_device(o):
        v = plane_peer(o)
        return (z * 2 + lax.rem(v, 2), v // 2)

    def z_device(o):
        return (lax.rem(z + o, nz) * 2 + core, g)

    barrier = pltpu.get_barrier_semaphore()
    for o in range(1, nf):
        pl.semaphore_signal(barrier, inc=1, device_id=(fibre_peer(o), g), device_id_type=MESH)
    for o in range(1, plane):
        pl.semaphore_signal(barrier, inc=1, device_id=plane_device(o), device_id_type=MESH)
    pl.semaphore_wait(barrier, nf + plane - 2)

    assert nf & (nf - 1) == 0
    near = [o for o in range(2, nf) if o < 4]
    far = [o for o in range(2, nf) if o >= 4]
    bounds = ((0, first), (first, rows))
    sends, owns = [], []
    for c, (low, high) in enumerate(bounds):
        here = fib.at[aligned(nf * low + f * (high - low), high - low), :]
        copies = {
            o: remote(
                field.at[low:high, pl.ds(pl.multiple_of(fibre_peer(o) * width, TILE), width)],
                here, a_send, a_recv, c * nf + o, (fibre_peer(o), g), start=False,
            )
            for o in range(1, nf)
        }

        if c == 0:
            for o in far + near + [1]:
                copies[o].start()
        sends.append(copies)
        own = pltpu.make_async_copy(
            field.at[low:high, pl.ds(pl.multiple_of(f * width, TILE), width)], here, own_sem.at[c]
        )
        own.start()
        owns.append(own)

    begin = pltpu.make_async_copy(start, held, own_sem.at[2])
    begin.start()
    begin.wait()
    held[...] = orth(contract(held[...], row_order(rows, first, nf), ((1,), (0,))), rows_ref)

    for o in [1] + near + far:
        sends[0][o].wait_send()
        sends[1][o].start()

    def summed(p):
        begin, size = sum(sizes[:p]), sizes[p]
        eighth = size // plane
        piece = eighth // nz
        at1 = 0 if p == 0 else r1.shape[1] - eighth
        at2 = 0 if p == 0 else r2.shape[1] - piece
        copies = [
            remote(part.at[aligned(begin + plane_peer(o) * eighth, eighth), :],
                   r1.at[o, at1:at1 + eighth, :], c_send, c_recv, 2 * p * plane + o, plane_device(o))
            for o in range(1, plane)
        ]
        yield
        for copy in copies:
            copy.wait()
        mine = begin + u * eighth
        total = part[aligned(mine, eighth), :]
        for o in range(1, plane):
            total += r1[o, at1:at1 + eighth, :]

        if p == 0:
            part[aligned(mine, eighth), :] = total
            copies = [
                remote(part.at[aligned(mine + lax.rem(z + o, nz) * piece, piece), :],
                       r2.at[o, at2:at2 + piece, :], z_send, z_recv, o, z_device(o))
                for o in range(1, nz)
            ]
            yield
            for copy in copies:
                copy.wait()
            last = mine + z * piece
            total = part[aligned(last, piece), :]
            for o in range(1, nz):
                total += r2[o, at2:at2 + piece, :]
            out[aligned(last, piece), :] = total * scale
            block = out.at[aligned(last, piece), :]
            copies = [
                remote(block, block, z_send, z_recv, nz + o, z_device(o)) for o in range(1, nz)
            ]
            yield
            for copy in copies:
                copy.wait()
        else:
            r3[z] = total
            copies = [
                remote(r3.at[z], r3.at[z], z_send, z_recv, 2 * nz + o, z_device(o))
                for o in range(1, nz)
            ]
            yield
            for copy in copies:
                copy.wait()
            total = r3[0]
            for n in range(1, nz):
                total += r3[n]
            out[aligned(mine, eighth), :] = total * scale

        block = out.at[aligned(mine, eighth), :]
        copies = [
            remote(block, block, c_send, c_recv, (2 * p + 1) * plane + o, plane_device(o))
            for o in range(1, plane)
        ]
        yield
        for copy in copies:
            copy.wait()

    going = []
    for c, (low, high) in enumerate(bounds):
        for copy in sends[c].values():
            copy.wait_recv()
        owns[c].wait()
        begin = sum(sizes[:c])
        base = begin
        end = nf * high // TILE
        for pair in range(nf * low // TILE, end, 2):
            top = min(pair + 2, end)
            strip = contract(fib[pair * TILE:top * TILE, :], fib[:top * TILE, :], ((1,), (1,)))
            for i in range(pair, top):
                for j in range(i + 1):
                    part[base:base + TILE, :] = strip[(i - pair) * TILE:(i - pair + 1) * TILE, j * TILE:(j + 1) * TILE]
                    base += TILE
        if base < begin + sizes[c]:
            part[base:begin + sizes[c], :] = jnp.zeros((begin + sizes[c] - base, TILE), jnp.float32)
        step = summed(c)
        next(step)
        going.append(step)
        if c == 0:
            next(step)
            next(step)
    going.reverse()
    while going:
        for step in list(going):
            try:
                next(step)
            except StopIteration:
                going.remove(step)
    for copy in sends[1].values():
        copy.wait_send()


def basis_kernel(nf, first, sizes, packed, fib, begin, basis, core, gram, held, rows_ref):
    order = fib.shape[0]
    split = nf * first // TILE
    base = 0
    for i in range(order // TILE):
        if i == split:
            base = sizes[0]
        for j in range(i + 1):
            block = packed[base:base + TILE, :]
            gram[i * TILE:(i + 1) * TILE, j * TILE:(j + 1) * TILE] = block
            if j < i:
                gram[j * TILE:(j + 1) * TILE, i * TILE:(i + 1) * TILE] = block.T
            base += TILE
    held[...] = begin[...]

    def iterate(step, carry):
        held[...] = orth(contract(held[...], gram[...], ((1,), (0,))), rows_ref)
        return carry

    lax.fori_loop(0, ITERS, iterate, 0)
    basis[...] = contract(held[...], row_order(order // nf, first, nf), ((1,), (1,)))
    core[...] = contract(held[...], fib[...], ((1,), (0,)))


def on_device(nf, ng, field, start):
    rows, columns = field.shape
    order, rank = start.shape
    width = columns // nf
    first = rows * 3 // 4 if rows % 32 == 0 else rows // 2
    blocks, early = order // TILE, nf * first // TILE
    unit = 8 * nf * ng
    counts = (early * (early + 1) // 2, blocks * (blocks + 1) // 2 - early * (early + 1) // 2)
    sizes = [-(-(n * TILE) // unit) * unit for n in counts]
    packed_rows = sum(sizes)
    plane, nz = 2 * ng, nf // 2
    vmem = pl.BlockSpec(memory_space=pltpu.VMEM)
    f32 = jnp.float32
    dma = pltpu.SemaphoreType.DMA
    fib, packed, begin = pl.pallas_call(
        functools.partial(gram_kernel, nf, ng, first, sizes, 1.0 / (columns * ng)),
        out_shape=(
            jax.ShapeDtypeStruct((order, width), f32),
            jax.ShapeDtypeStruct((packed_rows, TILE), f32),
            jax.ShapeDtypeStruct((rank, order), f32),
        ),
        in_specs=[pl.BlockSpec(memory_space=pltpu.HBM)] * 2,
        out_specs=(vmem, vmem, vmem),
        scratch_shapes=[
            pltpu.VMEM((packed_rows, TILE), f32),
            pltpu.VMEM((plane, packed_rows // plane, TILE), f32),
            pltpu.VMEM((nz, sizes[0] // plane // nz, TILE), f32),
            pltpu.VMEM((nz, sizes[1] // plane, TILE), f32),
            pltpu.VMEM((rank, 2 * rank), f32),
            dma((3,)),
            dma((2 * nf,)), dma((2 * nf,)),
            dma((4 * plane,)), dma((4 * plane,)),
            dma((3 * nz,)), dma((3 * nz,)),
        ],
        compiler_params=pltpu.CompilerParams(
            collective_id=0, has_side_effects=True, vmem_limit_bytes=50 * 2**20
        ),
        name="gram",
    )(field, start.T)
    basis, core = pl.pallas_call(
        functools.partial(basis_kernel, nf, first, sizes),
        out_shape=(
            jax.ShapeDtypeStruct((rank, order), f32),
            jax.ShapeDtypeStruct((rank, width), f32),
        ),
        in_specs=[vmem] * 3,
        out_specs=(vmem, vmem),
        scratch_shapes=[
            pltpu.VMEM((order, order), f32),
            pltpu.VMEM((rank, order), f32),
            pltpu.VMEM((rank, 2 * rank), f32),
        ],
        compiler_params=pltpu.CompilerParams(vmem_limit_bytes=48 * 2**20),
        name="basis",
    )(packed, fib, begin)
    return basis.T, core


def solution(mesh):
    nf, ng = mesh.shape["fibre"], mesh.shape["group"]
    return jax.shard_map(
        functools.partial(on_device, nf, ng),
        mesh=mesh,
        in_specs=(P("fibre", "group"), P()),
        out_specs=(P(), P(None, ("group", "fibre"))),
        check_vma=False,
    )
```

```python
import functools

import jax
import jax.numpy as jnp
from jax import lax
from jax.experimental import pallas as pl
from jax.experimental.pallas import tpu as pltpu
from jax.sharding import PartitionSpec as P

ITERS = 3
TILE = 128
MESH = pl.DeviceIdType.MESH
HIGHEST = lax.Precision.HIGHEST


def contract(a, b, dims):
    return lax.dot_general(
        a, b, (dims, ((), ())), precision=HIGHEST, preferred_element_type=jnp.float32
    )


def aligned(start, size):
    return pl.ds(pl.multiple_of(start, 8), size)


def inverse_factor(a, rows_ref):
    n = a.shape[0]
    eye = (
        lax.broadcasted_iota(jnp.int32, (n, n), 0) == lax.broadcasted_iota(jnp.int32, (n, n), 1)
    ).astype(jnp.float32)
    w = jnp.concatenate([a, eye], axis=1)
    for k in range(0, n, 8):
        left = n - k
        cols = [jnp.broadcast_to(w[:, k + j:k + j + 1], (left, 2 * n)) for j in range(8)]
        for j in range(8):
            pivot = cols[j][j:j + 1, :]
            inv = lax.rsqrt(pivot)
            inv = inv * (1.5 - 0.5 * pivot * inv * inv)
            row = w[j:j + 1, :] * inv
            rows_ref[k + j:k + j + 1, :] = row
            below = cols[j] * inv
            w = w - below * row
            for m in range(j + 1, 8):
                cols[m] = cols[m] - below * (cols[m][j:j + 1, :] * inv)
        w = w[8:, :]
    return rows_ref[:, n:]


def block_places(blocks):
    places = {}
    for pair in reversed(range(0, blocks, 2)):
        for i in range(pair, min(pair + 2, blocks)):
            for j in range(i + 1):
                places[i, j] = len(places) * TILE
    return places


def orth(matrix, rows_ref):
    inverse = inverse_factor(contract(matrix, matrix, ((1,), (1,))), rows_ref)
    return contract(inverse, matrix, ((1,), (0,)))


def gram_kernel(
    nf, ng, chunks, parts, scale, field, start, fib, out, held,
    part, r1, r2, r3, rows_ref, own_sem,
    a_send, a_recv, c_send, c_recv, g_send, g_recv, z_send, z_recv,
):
    f = lax.axis_index("fibre")
    g = lax.axis_index("group")
    nz = nf // 2
    core = lax.rem(f, 2)
    z = f // 2
    mate = f + 1 - 2 * core
    rows, width = field.shape[0], fib.shape[1]
    order = fib.shape[0]
    span = width // chunks

    def remote(src, dst, send, recv, slot, device):
        copy = pltpu.make_async_remote_copy(
            src_ref=src, dst_ref=dst, send_sem=send.at[slot], recv_sem=recv.at[slot],
            device_id=device, device_id_type=MESH,
        )
        copy.start()
        return copy

    def fibre_peer(o):
        return lax.rem(f + o, nf)

    def group_device(o):
        return (f, lax.rem(g + o, ng))

    def z_device(o):
        return (lax.rem(z + o, nz) * 2 + core, g)

    barrier = pltpu.get_barrier_semaphore()
    for o in range(1, nf):
        pl.semaphore_signal(barrier, inc=1, device_id=(fibre_peer(o), g), device_id_type=MESH)
    for o in range(1, ng):
        pl.semaphore_signal(barrier, inc=1, device_id=group_device(o), device_id_type=MESH)
    pl.semaphore_wait(barrier, nf + ng - 2)

    far_first = sorted(range(1, nf), key=lambda o: abs(o - nf // 2))
    sends = []
    owns = []
    for c in range(chunks):
        here = fib.at[aligned(f * rows, rows), c * span:(c + 1) * span]
        sends.append([
            remote(
                field.at[:, pl.ds(pl.multiple_of(fibre_peer(o) * width + c * span, TILE), span)],
                here, a_send, a_recv, c * nf + o, (fibre_peer(o), g),
            )
            for o in far_first
        ])
        own = pltpu.make_async_copy(
            field.at[:, pl.ds(pl.multiple_of(f * width + c * span, TILE), span)], here, own_sem.at[c]
        )
        own.start()
        owns.append(own)

    held[...] = orth(start[...], rows_ref)

    def summed(p, first, size):
        half = size // 2
        quarter = half // ng
        piece = quarter // nz
        mine = first + core * half
        other = first + (1 - core) * half
        copy = remote(part.at[aligned(other, half), :], r1.at[0:half, :] if p == 0 else r1.at[r1.shape[0] - half:, :],
                      c_send, c_recv, 2 * p, (mate, g))
        yield
        copy.wait()
        base1 = 0 if p == 0 else r1.shape[0] - half
        part[aligned(mine, half), :] += r1[base1:base1 + half, :]

        at2 = 0 if p == 0 else r2.shape[1] - quarter
        copies = [
            remote(part.at[aligned(mine + lax.rem(g + o, ng) * quarter, quarter), :],
                   r2.at[o, at2:at2 + quarter, :], g_send, g_recv, 2 * p * ng + o, group_device(o))
            for o in range(1, ng)
        ]
        yield
        for copy in copies:
            copy.wait()
        mine = mine + g * quarter
        total = part[aligned(mine, quarter), :]
        for o in range(1, ng):
            total += r2[o, at2:at2 + quarter, :]
        part[aligned(mine, quarter), :] = total

        at3 = 0 if p == 0 else r3.shape[1] - piece
        copies = [
            remote(part.at[aligned(mine + lax.rem(z + o, nz) * piece, piece), :],
                   r3.at[o, at3:at3 + piece, :], z_send, z_recv, 2 * p * nz + o, z_device(o))
            for o in range(1, nz)
        ]
        yield
        for copy in copies:
            copy.wait()
        last = mine + z * piece
        total = part[aligned(last, piece), :]
        for o in range(1, nz):
            total += r3[o, at3:at3 + piece, :]
        out[aligned(last, piece), :] = total * scale

        block = out.at[aligned(last, piece), :]
        copies = [
            remote(block, block, z_send, z_recv, (2 * p + 1) * nz + o, z_device(o))
            for o in range(1, nz)
        ]
        yield
        for copy in copies:
            copy.wait()
        block = out.at[aligned(mine, quarter), :]
        copies = [
            remote(block, block, g_send, g_recv, (2 * p + 1) * ng + o, group_device(o))
            for o in range(1, ng)
        ]
        yield
        for copy in copies:
            copy.wait()
        block = out.at[aligned(first + core * half, half), :]
        copy = remote(block, block, c_send, c_recv, 2 * p + 1, (mate, g))
        yield
        copy.wait()

    blocks = order // TILE
    places = block_places(blocks)
    filled = len(places) * TILE
    if filled < part.shape[0]:
        part[filled:, :] = jnp.zeros((part.shape[0] - filled, TILE), jnp.float32)
    sums = []
    for c in range(chunks):
        for copy in sends[c]:
            copy.wait_recv()
        owns[c].wait()
        columns = slice(c * span, (c + 1) * span)
        done = 0
        for pair in reversed(range(0, blocks, 2)):
            top = min(pair + 2, blocks)
            strip = contract(fib[pair * TILE:top * TILE, columns], fib[:top * TILE, columns], ((1,), (1,)))
            for i in range(pair, top):
                for j in range(i + 1):
                    block = strip[(i - pair) * TILE:(i - pair + 1) * TILE, j * TILE:(j + 1) * TILE]
                    at = slice(places[i, j], places[i, j] + TILE)
                    part[at, :] = block if c == 0 else part[at, :] + block
                    done += TILE
            if c == chunks - 1:
                ready = part.shape[0] if done == filled else done
                while len(sums) < len(parts) and sum(parts[len(sums)]) <= ready:
                    step = summed(len(sums), *parts[len(sums)])
                    next(step)
                    sums.append(step)
    going = list(sums)
    while going:
        for step in list(going):
            try:
                next(step)
            except StopIteration:
                going.remove(step)

    for copies in sends:
        for copy in copies:
            copy.wait_send()


def basis_kernel(packed, fib, begin, basis, core, gram, rows_ref):
    for (i, j), at in block_places(fib.shape[0] // TILE).items():
        block = packed[at:at + TILE, :]
        gram[i * TILE:(i + 1) * TILE, j * TILE:(j + 1) * TILE] = block
        if j < i:
            gram[j * TILE:(j + 1) * TILE, i * TILE:(i + 1) * TILE] = block.T
    basis[...] = begin[...]

    def iterate(step, carry):
        basis[...] = orth(contract(basis[...], gram[...], ((1,), (0,))), rows_ref)
        return carry

    lax.fori_loop(0, ITERS, iterate, 0)
    core[...] = contract(basis[...], fib[...], ((1,), (0,)))


def on_device(nf, ng, field, start):
    rows, columns = field.shape
    order, rank = start.shape
    width = columns // nf
    chunks = 4
    blocks = order // TILE
    unit = 8 * nf * ng
    units = -(-(blocks * (blocks + 1) // 2 * TILE) // unit)
    sizes = [n * unit for n in (units - units // 2, units // 2) if n]
    parts = [(sum(sizes[:p]), size) for p, size in enumerate(sizes)]
    packed_rows = sum(sizes)
    vmem = pl.BlockSpec(memory_space=pltpu.VMEM)
    f32 = jnp.float32
    dma = pltpu.SemaphoreType.DMA
    fib, packed, begin = pl.pallas_call(
        functools.partial(gram_kernel, nf, ng, chunks, parts, 1.0 / (columns * ng)),
        out_shape=(
            jax.ShapeDtypeStruct((order, width), f32),
            jax.ShapeDtypeStruct((packed_rows, TILE), f32),
            jax.ShapeDtypeStruct((rank, order), f32),
        ),
        in_specs=[pl.BlockSpec(memory_space=pltpu.HBM), vmem],
        out_specs=(vmem, vmem, vmem),
        scratch_shapes=[
            pltpu.VMEM((packed_rows, TILE), f32),
            pltpu.VMEM((packed_rows // 2, TILE), f32),
            pltpu.VMEM((ng, packed_rows // 2 // ng, TILE), f32),
            pltpu.VMEM((nf // 2, packed_rows // nf // ng, TILE), f32),
            pltpu.VMEM((rank, 2 * rank), f32),
            dma((chunks,)),
            dma((chunks * nf,)), dma((chunks * nf,)),
            dma((4,)), dma((4,)),
            dma((4 * ng,)), dma((4 * ng,)),
            dma((2 * nf,)), dma((2 * nf,)),
        ],
        compiler_params=pltpu.CompilerParams(
            collective_id=0, has_side_effects=True, vmem_limit_bytes=50 * 2**20
        ),
        name="gram",
    )(field, start.T)
    basis, core = pl.pallas_call(
        basis_kernel,
        out_shape=(
            jax.ShapeDtypeStruct((rank, order), f32),
            jax.ShapeDtypeStruct((rank, width), f32),
        ),
        in_specs=[vmem] * 3,
        out_specs=(vmem, vmem),
        scratch_shapes=[pltpu.VMEM((order, order), f32), pltpu.VMEM((rank, 2 * rank), f32)],
        compiler_params=pltpu.CompilerParams(vmem_limit_bytes=48 * 2**20),
        name="basis",
    )(packed, fib, begin)
    return basis.T, core


def solution(mesh):
    nf, ng = mesh.shape["fibre"], mesh.shape["group"]
    return jax.shard_map(
        functools.partial(on_device, nf, ng),
        mesh=mesh,
        in_specs=(P("fibre", "group"), P()),
        out_specs=(P(), P(None, ("group", "fibre"))),
        check_vma=False,
    )
```

```python
import functools

import jax
import jax.numpy as jnp
from jax import lax
from jax.experimental import pallas as pl
from jax.experimental.pallas import tpu as pltpu
from jax.sharding import PartitionSpec as P

ITERS = 3
TILE = 128
MESH = pl.DeviceIdType.MESH
HIGHEST = lax.Precision.HIGHEST


def contract(a, b, dims):
    return lax.dot_general(
        a, b, (dims, ((), ())), precision=HIGHEST, preferred_element_type=jnp.float32
    )


def aligned(start, size):
    return pl.ds(pl.multiple_of(start, 8), size)


def inverse_factor(a, rows_ref):
    n = a.shape[0]
    eye = (
        lax.broadcasted_iota(jnp.int32, (n, n), 0) == lax.broadcasted_iota(jnp.int32, (n, n), 1)
    ).astype(jnp.float32)
    w = jnp.concatenate([a, eye], axis=1)
    for k in range(0, n, 8):
        left = n - k
        cols = [jnp.broadcast_to(w[:, k + j:k + j + 1], (left, 2 * n)) for j in range(8)]
        for j in range(8):
            pivot = cols[j][j:j + 1, :]
            inv = lax.rsqrt(pivot)
            inv = inv * (1.5 - 0.5 * pivot * inv * inv)
            row = w[j:j + 1, :] * inv
            rows_ref[k + j:k + j + 1, :] = row
            below = cols[j] * inv
            w = w - below * row
            for m in range(j + 1, 8):
                cols[m] = cols[m] - below * (cols[m][j:j + 1, :] * inv)
        w = w[8:, :]
    return rows_ref[:, n:]


def block_places(blocks):
    places = {}
    for pair in reversed(range(0, blocks, 2)):
        for i in range(pair, min(pair + 2, blocks)):
            for j in range(i + 1):
                places[i, j] = len(places) * TILE
    return places


def orth(matrix, rows_ref):
    inverse = inverse_factor(contract(matrix, matrix, ((1,), (1,))), rows_ref)
    return contract(inverse, matrix, ((1,), (0,)))


def gram_kernel(
    nf, ng, chunks, parts, scale, field, start, fib, out, held,
    part, r1, r2, r3, rows_ref, own_sem,
    a_send, a_recv, c_send, c_recv, g_send, g_recv, z_send, z_recv,
):
    f = lax.axis_index("fibre")
    g = lax.axis_index("group")
    nz = nf // 2
    core = lax.rem(f, 2)
    z = f // 2
    mate = f + 1 - 2 * core
    rows, width = field.shape[0], fib.shape[1]
    order = fib.shape[0]
    span = width // chunks

    def remote(src, dst, send, recv, slot, device):
        copy = pltpu.make_async_remote_copy(
            src_ref=src, dst_ref=dst, send_sem=send.at[slot], recv_sem=recv.at[slot],
            device_id=device, device_id_type=MESH,
        )
        copy.start()
        return copy

    def fibre_peer(o):
        return lax.rem(f + o, nf)

    def group_device(o):
        return (f, lax.rem(g + o, ng))

    def z_device(o):
        return (lax.rem(z + o, nz) * 2 + core, g)

    barrier = pltpu.get_barrier_semaphore()
    for o in range(1, nf):
        pl.semaphore_signal(barrier, inc=1, device_id=(fibre_peer(o), g), device_id_type=MESH)
    for o in range(1, ng):
        pl.semaphore_signal(barrier, inc=1, device_id=group_device(o), device_id_type=MESH)
    pl.semaphore_wait(barrier, nf + ng - 2)

    far_first = sorted(range(1, nf), key=lambda o: abs(o - nf // 2))
    sends = []
    owns = []
    for c in range(chunks):
        here = fib.at[aligned(f * rows, rows), c * span:(c + 1) * span]
        sends.append([
            remote(
                field.at[:, pl.ds(pl.multiple_of(fibre_peer(o) * width + c * span, TILE), span)],
                here, a_send, a_recv, c * nf + o, (fibre_peer(o), g),
            )
            for o in far_first
        ])
        own = pltpu.make_async_copy(
            field.at[:, pl.ds(pl.multiple_of(f * width + c * span, TILE), span)], here, own_sem.at[c]
        )
        own.start()
        owns.append(own)

    held[...] = orth(start[...], rows_ref)

    def summed(p, first, size):
        half = size // 2
        quarter = half // ng
        piece = quarter // nz
        mine = first + core * half
        other = first + (1 - core) * half
        copy = remote(part.at[aligned(other, half), :], r1.at[0:half, :] if p == 0 else r1.at[r1.shape[0] - half:, :],
                      c_send, c_recv, 2 * p, (mate, g))
        yield
        copy.wait()
        base1 = 0 if p == 0 else r1.shape[0] - half
        part[aligned(mine, half), :] += r1[base1:base1 + half, :]

        at2 = 0 if p == 0 else r2.shape[1] - quarter
        copies = [
            remote(part.at[aligned(mine + lax.rem(g + o, ng) * quarter, quarter), :],
                   r2.at[o, at2:at2 + quarter, :], g_send, g_recv, 2 * p * ng + o, group_device(o))
            for o in range(1, ng)
        ]
        yield
        for copy in copies:
            copy.wait()
        mine = mine + g * quarter
        total = part[aligned(mine, quarter), :]
        for o in range(1, ng):
            total += r2[o, at2:at2 + quarter, :]
        part[aligned(mine, quarter), :] = total

        at3 = 0 if p == 0 else r3.shape[1] - piece
        copies = [
            remote(part.at[aligned(mine + lax.rem(z + o, nz) * piece, piece), :],
                   r3.at[o, at3:at3 + piece, :], z_send, z_recv, 2 * p * nz + o, z_device(o))
            for o in range(1, nz)
        ]
        yield
        for copy in copies:
            copy.wait()
        last = mine + z * piece
        total = part[aligned(last, piece), :]
        for o in range(1, nz):
            total += r3[o, at3:at3 + piece, :]
        out[aligned(last, piece), :] = total * scale

        block = out.at[aligned(last, piece), :]
        copies = [
            remote(block, block, z_send, z_recv, (2 * p + 1) * nz + o, z_device(o))
            for o in range(1, nz)
        ]
        yield
        for copy in copies:
            copy.wait()
        block = out.at[aligned(mine, quarter), :]
        copies = [
            remote(block, block, g_send, g_recv, (2 * p + 1) * ng + o, group_device(o))
            for o in range(1, ng)
        ]
        yield
        for copy in copies:
            copy.wait()
        block = out.at[aligned(first + core * half, half), :]
        copy = remote(block, block, c_send, c_recv, 2 * p + 1, (mate, g))
        yield
        copy.wait()

    blocks = order // TILE
    places = block_places(blocks)
    filled = len(places) * TILE
    if filled < part.shape[0]:
        part[filled:, :] = jnp.zeros((part.shape[0] - filled, TILE), jnp.float32)
    sums = []
    for c in range(chunks):
        for copy in sends[c]:
            copy.wait_recv()
        owns[c].wait()
        columns = slice(c * span, (c + 1) * span)
        done = 0
        for pair in reversed(range(0, blocks, 2)):
            top = min(pair + 2, blocks)
            strip = contract(fib[pair * TILE:top * TILE, columns], fib[:top * TILE, columns], ((1,), (1,)))
            for i in range(pair, top):
                for j in range(i + 1):
                    block = strip[(i - pair) * TILE:(i - pair + 1) * TILE, j * TILE:(j + 1) * TILE]
                    at = slice(places[i, j], places[i, j] + TILE)
                    part[at, :] = block if c == 0 else part[at, :] + block
                    done += TILE
            if c == chunks - 1:
                ready = part.shape[0] if done == filled else done
                while len(sums) < len(parts) and sum(parts[len(sums)]) <= ready:
                    step = summed(len(sums), *parts[len(sums)])
                    next(step)
                    sums.append(step)
    going = list(sums)
    while going:
        for step in list(going):
            try:
                next(step)
            except StopIteration:
                going.remove(step)

    for copies in sends:
        for copy in copies:
            copy.wait_send()


def basis_kernel(packed, fib, begin, basis, core, gram, held, rows_ref):
    for (i, j), at in block_places(fib.shape[0] // TILE).items():
        block = packed[at:at + TILE, :]
        gram[i * TILE:(i + 1) * TILE, j * TILE:(j + 1) * TILE] = block
        if j < i:
            gram[j * TILE:(j + 1) * TILE, i * TILE:(i + 1) * TILE] = block.T
    held[...] = contract(begin[...], gram[...], ((1,), (0,)))

    def iterate(step, carry):
        matrix = held[...]
        inner = contract(matrix, matrix, ((1,), (1,)))
        after = contract(matrix, gram[...], ((1,), (0,)))
        held[...] = contract(inverse_factor(inner, rows_ref), after, ((1,), (0,)))
        return carry

    lax.fori_loop(0, ITERS - 1, iterate, 0)
    matrix = held[...]
    inner = contract(matrix, matrix, ((1,), (1,)))
    after = contract(matrix, fib[...], ((1,), (0,)))
    inverse = inverse_factor(inner, rows_ref)
    basis[...] = contract(inverse, matrix, ((1,), (0,)))
    core[...] = contract(inverse, after, ((1,), (0,)))


def on_device(nf, ng, field, start):
    rows, columns = field.shape
    order, rank = start.shape
    width = columns // nf
    chunks = 4
    blocks = order // TILE
    unit = 8 * nf * ng
    units = -(-(blocks * (blocks + 1) // 2 * TILE) // unit)
    sizes = [n * unit for n in (units - units // 2, units // 2) if n]
    parts = [(sum(sizes[:p]), size) for p, size in enumerate(sizes)]
    packed_rows = sum(sizes)
    vmem = pl.BlockSpec(memory_space=pltpu.VMEM)
    f32 = jnp.float32
    dma = pltpu.SemaphoreType.DMA
    fib, packed, begin = pl.pallas_call(
        functools.partial(gram_kernel, nf, ng, chunks, parts, 1.0 / (columns * ng)),
        out_shape=(
            jax.ShapeDtypeStruct((order, width), f32),
            jax.ShapeDtypeStruct((packed_rows, TILE), f32),
            jax.ShapeDtypeStruct((rank, order), f32),
        ),
        in_specs=[pl.BlockSpec(memory_space=pltpu.HBM), vmem],
        out_specs=(vmem, vmem, vmem),
        scratch_shapes=[
            pltpu.VMEM((packed_rows, TILE), f32),
            pltpu.VMEM((packed_rows // 2, TILE), f32),
            pltpu.VMEM((ng, packed_rows // 2 // ng, TILE), f32),
            pltpu.VMEM((nf // 2, packed_rows // nf // ng, TILE), f32),
            pltpu.VMEM((rank, 2 * rank), f32),
            dma((chunks,)),
            dma((chunks * nf,)), dma((chunks * nf,)),
            dma((4,)), dma((4,)),
            dma((4 * ng,)), dma((4 * ng,)),
            dma((2 * nf,)), dma((2 * nf,)),
        ],
        compiler_params=pltpu.CompilerParams(
            collective_id=0, has_side_effects=True, vmem_limit_bytes=50 * 2**20
        ),
        name="gram",
    )(field, start.T)
    basis, core = pl.pallas_call(
        basis_kernel,
        out_shape=(
            jax.ShapeDtypeStruct((rank, order), f32),
            jax.ShapeDtypeStruct((rank, width), f32),
        ),
        in_specs=[vmem] * 3,
        out_specs=(vmem, vmem),
        scratch_shapes=[
            pltpu.VMEM((order, order), f32),
            pltpu.VMEM((rank, order), f32),
            pltpu.VMEM((rank, 2 * rank), f32),
        ],
        compiler_params=pltpu.CompilerParams(vmem_limit_bytes=48 * 2**20),
        name="basis",
    )(packed, fib, begin)
    return basis.T, core


def solution(mesh):
    nf, ng = mesh.shape["fibre"], mesh.shape["group"]
    return jax.shard_map(
        functools.partial(on_device, nf, ng),
        mesh=mesh,
        in_specs=(P("fibre", "group"), P()),
        out_specs=(P(), P(None, ("group", "fibre"))),
        check_vma=False,
    )
```

```python
import functools

import jax
import jax.numpy as jnp
from jax import lax
from jax.experimental import pallas as pl
from jax.experimental.pallas import tpu as pltpu
from jax.sharding import PartitionSpec as P

ITERS = 3
TILE = 128
MESH = pl.DeviceIdType.MESH
HIGHEST = lax.Precision.HIGHEST


def contract(a, b, dims):
    return lax.dot_general(
        a, b, (dims, ((), ())), precision=HIGHEST, preferred_element_type=jnp.float32
    )


def aligned(start, size):
    return pl.ds(pl.multiple_of(start, 8), size)


def inverse_factor(a, rows_ref):
    n = a.shape[0]
    eye = (
        lax.broadcasted_iota(jnp.int32, (n, n), 0) == lax.broadcasted_iota(jnp.int32, (n, n), 1)
    ).astype(jnp.float32)
    w = jnp.concatenate([a, eye], axis=1)
    for k in range(0, n, 8):
        left = n - k
        cols = [jnp.broadcast_to(w[:, k + j:k + j + 1], (left, 2 * n)) for j in range(8)]
        for j in range(8):
            pivot = cols[j][j:j + 1, :]
            inv = lax.rsqrt(pivot)
            inv = inv * (1.5 - 0.5 * pivot * inv * inv)
            row = w[j:j + 1, :] * inv
            rows_ref[k + j:k + j + 1, :] = row
            below = cols[j] * inv
            w = w - below * row
            for m in range(j + 1, 8):
                cols[m] = cols[m] - below * (cols[m][j:j + 1, :] * inv)
        w = w[8:, :]
    return rows_ref[:, n:]


def block_places(blocks):
    places = {}
    for pair in reversed(range(0, blocks, 2)):
        for i in range(pair, min(pair + 2, blocks)):
            for j in range(i + 1):
                places[i, j] = len(places) * TILE
    return places


def orth(matrix, rows_ref):
    inverse = inverse_factor(contract(matrix, matrix, ((1,), (1,))), rows_ref)
    return contract(inverse, matrix, ((1,), (0,)))


def gram_kernel(
    nf, ng, chunks, parts, scale, field, start, fib, out, held,
    part, r1, r2, r3, rows_ref, own_sem,
    a_send, a_recv, c_send, c_recv, g_send, g_recv, z_send, z_recv,
):
    f = lax.axis_index("fibre")
    g = lax.axis_index("group")
    nz = nf // 2
    core = lax.rem(f, 2)
    z = f // 2
    mate = f + 1 - 2 * core
    rows, width = field.shape[0], fib.shape[1]
    order = fib.shape[0]
    span = width // chunks

    def remote(src, dst, send, recv, slot, device, start=True):
        copy = pltpu.make_async_remote_copy(
            src_ref=src, dst_ref=dst, send_sem=send.at[slot], recv_sem=recv.at[slot],
            device_id=device, device_id_type=MESH,
        )
        if start:
            copy.start()
        return copy

    def fibre_peer(o):
        return lax.rem(f + o, nf)

    def group_device(o):
        return (f, lax.rem(g + o, ng))

    def z_device(o):
        return (lax.rem(z + o, nz) * 2 + core, g)

    barrier = pltpu.get_barrier_semaphore()
    for o in range(1, nf):
        pl.semaphore_signal(barrier, inc=1, device_id=(fibre_peer(o), g), device_id_type=MESH)
    for o in range(1, ng):
        pl.semaphore_signal(barrier, inc=1, device_id=group_device(o), device_id_type=MESH)
    pl.semaphore_wait(barrier, nf + ng - 2)

    far_first = sorted(range(1, nf), key=lambda o: abs(o - nf // 2))
    ahead = 2
    sends = []
    owns = []
    for c in range(chunks):
        here = fib.at[aligned(f * rows, rows), c * span:(c + 1) * span]
        sends.append([
            remote(
                field.at[:, pl.ds(pl.multiple_of(fibre_peer(o) * width + c * span, TILE), span)],
                here, a_send, a_recv, c * nf + o, (fibre_peer(o), g), start=c < ahead,
            )
            for o in far_first
        ])
        own = pltpu.make_async_copy(
            field.at[:, pl.ds(pl.multiple_of(f * width + c * span, TILE), span)], here, own_sem.at[c]
        )
        own.start()
        owns.append(own)

    held[...] = orth(start[...], rows_ref)

    def summed(p, first, size):
        half = size // 2
        quarter = half // ng
        piece = quarter // nz
        mine = first + core * half
        other = first + (1 - core) * half
        copy = remote(part.at[aligned(other, half), :], r1.at[0:half, :] if p == 0 else r1.at[r1.shape[0] - half:, :],
                      c_send, c_recv, 2 * p, (mate, g))
        yield
        copy.wait()
        base1 = 0 if p == 0 else r1.shape[0] - half
        part[aligned(mine, half), :] += r1[base1:base1 + half, :]

        at2 = 0 if p == 0 else r2.shape[1] - quarter
        copies = [
            remote(part.at[aligned(mine + lax.rem(g + o, ng) * quarter, quarter), :],
                   r2.at[o, at2:at2 + quarter, :], g_send, g_recv, 2 * p * ng + o, group_device(o))
            for o in range(1, ng)
        ]
        yield
        for copy in copies:
            copy.wait()
        mine = mine + g * quarter
        total = part[aligned(mine, quarter), :]
        for o in range(1, ng):
            total += r2[o, at2:at2 + quarter, :]
        part[aligned(mine, quarter), :] = total

        at3 = 0 if p == 0 else r3.shape[1] - piece
        copies = [
            remote(part.at[aligned(mine + lax.rem(z + o, nz) * piece, piece), :],
                   r3.at[o, at3:at3 + piece, :], z_send, z_recv, 2 * p * nz + o, z_device(o))
            for o in range(1, nz)
        ]
        yield
        for copy in copies:
            copy.wait()
        last = mine + z * piece
        total = part[aligned(last, piece), :]
        for o in range(1, nz):
            total += r3[o, at3:at3 + piece, :]
        out[aligned(last, piece), :] = total * scale

        block = out.at[aligned(last, piece), :]
        copies = [
            remote(block, block, z_send, z_recv, (2 * p + 1) * nz + o, z_device(o))
            for o in range(1, nz)
        ]
        yield
        for copy in copies:
            copy.wait()
        block = out.at[aligned(mine, quarter), :]
        copies = [
            remote(block, block, g_send, g_recv, (2 * p + 1) * ng + o, group_device(o))
            for o in range(1, ng)
        ]
        yield
        for copy in copies:
            copy.wait()
        block = out.at[aligned(first + core * half, half), :]
        copy = remote(block, block, c_send, c_recv, 2 * p + 1, (mate, g))
        yield
        copy.wait()

    blocks = order // TILE
    places = block_places(blocks)
    filled = len(places) * TILE
    if filled < part.shape[0]:
        part[filled:, :] = jnp.zeros((part.shape[0] - filled, TILE), jnp.float32)
    sums = []
    for c in range(chunks):
        if c + ahead < chunks:
            for now, later in reversed(list(zip(sends[c], sends[c + ahead]))):
                now.wait_send()
                later.start()
        for copy in sends[c]:
            copy.wait_recv()
        owns[c].wait()
        columns = slice(c * span, (c + 1) * span)
        done = 0
        for pair in reversed(range(0, blocks, 2)):
            top = min(pair + 2, blocks)
            strip = contract(fib[pair * TILE:top * TILE, columns], fib[:top * TILE, columns], ((1,), (1,)))
            for i in range(pair, top):
                for j in range(i + 1):
                    block = strip[(i - pair) * TILE:(i - pair + 1) * TILE, j * TILE:(j + 1) * TILE]
                    at = slice(places[i, j], places[i, j] + TILE)
                    part[at, :] = block if c == 0 else part[at, :] + block
                    done += TILE
            if c == chunks - 1:
                ready = part.shape[0] if done == filled else done
                while len(sums) < len(parts) and sum(parts[len(sums)]) <= ready:
                    step = summed(len(sums), *parts[len(sums)])
                    next(step)
                    sums.append(step)
    going = list(sums)
    while going:
        for step in list(going):
            try:
                next(step)
            except StopIteration:
                going.remove(step)

    for copies in sends[-ahead:]:
        for copy in copies:
            copy.wait_send()


def basis_kernel(packed, fib, begin, basis, core, gram, held, rows_ref):
    for (i, j), at in block_places(fib.shape[0] // TILE).items():
        block = packed[at:at + TILE, :]
        gram[i * TILE:(i + 1) * TILE, j * TILE:(j + 1) * TILE] = block
        if j < i:
            gram[j * TILE:(j + 1) * TILE, i * TILE:(i + 1) * TILE] = block.T
    held[...] = contract(begin[...], gram[...], ((1,), (0,)))

    def iterate(step, carry):
        matrix = held[...]
        inner = contract(matrix, matrix, ((1,), (1,)))
        after = contract(matrix, gram[...], ((1,), (0,)))
        held[...] = contract(inverse_factor(inner, rows_ref), after, ((1,), (0,)))
        return carry

    lax.fori_loop(0, ITERS - 1, iterate, 0)
    matrix = held[...]
    inner = contract(matrix, matrix, ((1,), (1,)))
    after = contract(matrix, fib[...], ((1,), (0,)))
    inverse = inverse_factor(inner, rows_ref)
    basis[...] = contract(inverse, matrix, ((1,), (0,)))
    core[...] = contract(inverse, after, ((1,), (0,)))


def on_device(nf, ng, field, start):
    rows, columns = field.shape
    order, rank = start.shape
    width = columns // nf
    chunks = 4
    blocks = order // TILE
    unit = 8 * nf * ng
    units = -(-(blocks * (blocks + 1) // 2 * TILE) // unit)
    sizes = [n * unit for n in (units - units // 2, units // 2) if n]
    parts = [(sum(sizes[:p]), size) for p, size in enumerate(sizes)]
    packed_rows = sum(sizes)
    vmem = pl.BlockSpec(memory_space=pltpu.VMEM)
    f32 = jnp.float32
    dma = pltpu.SemaphoreType.DMA
    fib, packed, begin = pl.pallas_call(
        functools.partial(gram_kernel, nf, ng, chunks, parts, 1.0 / (columns * ng)),
        out_shape=(
            jax.ShapeDtypeStruct((order, width), f32),
            jax.ShapeDtypeStruct((packed_rows, TILE), f32),
            jax.ShapeDtypeStruct((rank, order), f32),
        ),
        in_specs=[pl.BlockSpec(memory_space=pltpu.HBM), vmem],
        out_specs=(vmem, vmem, vmem),
        scratch_shapes=[
            pltpu.VMEM((packed_rows, TILE), f32),
            pltpu.VMEM((packed_rows // 2, TILE), f32),
            pltpu.VMEM((ng, packed_rows // 2 // ng, TILE), f32),
            pltpu.VMEM((nf // 2, packed_rows // nf // ng, TILE), f32),
            pltpu.VMEM((rank, 2 * rank), f32),
            dma((chunks,)),
            dma((chunks * nf,)), dma((chunks * nf,)),
            dma((4,)), dma((4,)),
            dma((4 * ng,)), dma((4 * ng,)),
            dma((2 * nf,)), dma((2 * nf,)),
        ],
        compiler_params=pltpu.CompilerParams(
            collective_id=0, has_side_effects=True, vmem_limit_bytes=50 * 2**20
        ),
        name="gram",
    )(field, start.T)
    basis, core = pl.pallas_call(
        basis_kernel,
        out_shape=(
            jax.ShapeDtypeStruct((rank, order), f32),
            jax.ShapeDtypeStruct((rank, width), f32),
        ),
        in_specs=[vmem] * 3,
        out_specs=(vmem, vmem),
        scratch_shapes=[
            pltpu.VMEM((order, order), f32),
            pltpu.VMEM((rank, order), f32),
            pltpu.VMEM((rank, 2 * rank), f32),
        ],
        compiler_params=pltpu.CompilerParams(vmem_limit_bytes=48 * 2**20),
        name="basis",
    )(packed, fib, begin)
    return basis.T, core


def solution(mesh):
    nf, ng = mesh.shape["fibre"], mesh.shape["group"]
    return jax.shard_map(
        functools.partial(on_device, nf, ng),
        mesh=mesh,
        in_specs=(P("fibre", "group"), P()),
        out_specs=(P(), P(None, ("group", "fibre"))),
        check_vma=False,
    )
```

```python
import functools

import jax
import jax.numpy as jnp
from jax import lax
from jax.experimental import pallas as pl
from jax.experimental.pallas import tpu as pltpu
from jax.sharding import PartitionSpec as P

ITERS = 3
TILE = 128
MESH = pl.DeviceIdType.MESH
HIGHEST = lax.Precision.HIGHEST


def contract(a, b, dims):
    return lax.dot_general(
        a, b, (dims, ((), ())), precision=HIGHEST, preferred_element_type=jnp.float32
    )


def aligned(start, size):
    return pl.ds(pl.multiple_of(start, 8), size)


def inverse_factor(a, rows_ref):
    n = a.shape[0]
    eye = (
        lax.broadcasted_iota(jnp.int32, (n, n), 0) == lax.broadcasted_iota(jnp.int32, (n, n), 1)
    ).astype(jnp.float32)
    w = jnp.concatenate([a, eye], axis=1)
    for k in range(0, n, 8):
        left = n - k
        cols = [jnp.broadcast_to(w[:, k + j:k + j + 1], (left, 2 * n)) for j in range(8)]
        for j in range(8):
            pivot = cols[j][j:j + 1, :]
            inv = lax.rsqrt(pivot)
            inv = inv * (1.5 - 0.5 * pivot * inv * inv)
            row = w[j:j + 1, :] * inv
            rows_ref[k + j:k + j + 1, :] = row
            below = cols[j] * inv
            w = w - below * row
            for m in range(j + 1, 8):
                cols[m] = cols[m] - below * (cols[m][j:j + 1, :] * inv)
        w = w[8:, :]
    return rows_ref[:, n:]


def block_places(blocks):
    places = {}
    for pair in reversed(range(0, blocks, 2)):
        for i in range(pair, min(pair + 2, blocks)):
            for j in range(i + 1):
                places[i, j] = len(places) * TILE
    return places


def orth(matrix, rows_ref):
    inverse = inverse_factor(contract(matrix, matrix, ((1,), (1,))), rows_ref)
    return contract(inverse, matrix, ((1,), (0,)))


def gram_kernel(
    nf, ng, chunks, parts, scale, field, start, fib, out, held,
    part, r1, r2, rows_ref, own_sem,
    a_send, a_recv, c_send, c_recv, z_send, z_recv,
):
    f = lax.axis_index("fibre")
    g = lax.axis_index("group")
    nz = nf // 2
    core = lax.rem(f, 2)
    z = f // 2
    plane = 2 * ng
    u = g * 2 + core
    rows, width = field.shape[0], fib.shape[1]
    order = fib.shape[0]
    span = width // chunks

    def remote(src, dst, send, recv, slot, device):
        copy = pltpu.make_async_remote_copy(
            src_ref=src, dst_ref=dst, send_sem=send.at[slot], recv_sem=recv.at[slot],
            device_id=device, device_id_type=MESH,
        )
        copy.start()
        return copy

    def fibre_peer(o):
        return lax.rem(f + o, nf)

    def plane_peer(o):
        return lax.rem(u + o, plane)

    def plane_device(o):
        v = plane_peer(o)
        return (z * 2 + lax.rem(v, 2), v // 2)

    def z_device(o):
        return (lax.rem(z + o, nz) * 2 + core, g)

    barrier = pltpu.get_barrier_semaphore()
    for o in range(1, nf):
        pl.semaphore_signal(barrier, inc=1, device_id=(fibre_peer(o), g), device_id_type=MESH)
    for o in range(1, plane):
        pl.semaphore_signal(barrier, inc=1, device_id=plane_device(o), device_id_type=MESH)
    pl.semaphore_wait(barrier, nf + plane - 2)

    far_first = sorted(range(1, nf), key=lambda o: abs(o - nf // 2))
    sends = []
    owns = []
    for c in range(chunks):
        here = fib.at[aligned(f * rows, rows), c * span:(c + 1) * span]
        sends.append([
            remote(
                field.at[:, pl.ds(pl.multiple_of(fibre_peer(o) * width + c * span, TILE), span)],
                here, a_send, a_recv, c * nf + o, (fibre_peer(o), g),
            )
            for o in far_first
        ])
        own = pltpu.make_async_copy(
            field.at[:, pl.ds(pl.multiple_of(f * width + c * span, TILE), span)], here, own_sem.at[c]
        )
        own.start()
        owns.append(own)

    held[...] = orth(start[...], rows_ref)

    def summed(p, first, size):
        eighth = size // plane
        piece = eighth // nz
        at1 = 0 if p == 0 else r1.shape[1] - eighth
        at2 = 0 if p == 0 else r2.shape[1] - piece
        copies = [
            remote(part.at[aligned(first + plane_peer(o) * eighth, eighth), :],
                   r1.at[o, at1:at1 + eighth, :], c_send, c_recv, 2 * p * plane + o, plane_device(o))
            for o in range(1, plane)
        ]
        yield
        for copy in copies:
            copy.wait()
        mine = first + u * eighth
        total = part[aligned(mine, eighth), :]
        for o in range(1, plane):
            total += r1[o, at1:at1 + eighth, :]
        part[aligned(mine, eighth), :] = total
        copies = [
            remote(part.at[aligned(mine + lax.rem(z + o, nz) * piece, piece), :],
                   r2.at[o, at2:at2 + piece, :], z_send, z_recv, 2 * p * nz + o, z_device(o))
            for o in range(1, nz)
        ]
        yield
        for copy in copies:
            copy.wait()
        last = mine + z * piece
        total = part[aligned(last, piece), :]
        for o in range(1, nz):
            total += r2[o, at2:at2 + piece, :]
        out[aligned(last, piece), :] = total * scale
        block = out.at[aligned(last, piece), :]
        copies = [
            remote(block, block, z_send, z_recv, (2 * p + 1) * nz + o, z_device(o))
            for o in range(1, nz)
        ]
        yield
        for copy in copies:
            copy.wait()
        block = out.at[aligned(mine, eighth), :]
        copies = [
            remote(block, block, c_send, c_recv, (2 * p + 1) * plane + o, plane_device(o))
            for o in range(1, plane)
        ]
        yield
        for copy in copies:
            copy.wait()

    blocks = order // TILE
    places = block_places(blocks)
    filled = len(places) * TILE
    if filled < part.shape[0]:
        part[filled:, :] = jnp.zeros((part.shape[0] - filled, TILE), jnp.float32)
    sums = []
    for c in range(chunks):
        for copy in sends[c]:
            copy.wait_recv()
        owns[c].wait()
        columns = slice(c * span, (c + 1) * span)
        done = 0
        for pair in reversed(range(0, blocks, 2)):
            top = min(pair + 2, blocks)
            strip = contract(fib[pair * TILE:top * TILE, columns], fib[:top * TILE, columns], ((1,), (1,)))
            for i in range(pair, top):
                for j in range(i + 1):
                    block = strip[(i - pair) * TILE:(i - pair + 1) * TILE, j * TILE:(j + 1) * TILE]
                    at = slice(places[i, j], places[i, j] + TILE)
                    part[at, :] = block if c == 0 else part[at, :] + block
                    done += TILE
            if c == chunks - 1:
                ready = part.shape[0] if done == filled else done
                while len(sums) < len(parts) and sum(parts[len(sums)]) <= ready:
                    step = summed(len(sums), *parts[len(sums)])
                    next(step)
                    sums.append(step)
    going = list(sums)
    while going:
        for step in list(going):
            try:
                next(step)
            except StopIteration:
                going.remove(step)

    for copies in sends:
        for copy in copies:
            copy.wait_send()


def basis_kernel(packed, fib, begin, basis, core, gram, held, rows_ref):
    for (i, j), at in block_places(fib.shape[0] // TILE).items():
        block = packed[at:at + TILE, :]
        gram[i * TILE:(i + 1) * TILE, j * TILE:(j + 1) * TILE] = block
        if j < i:
            gram[j * TILE:(j + 1) * TILE, i * TILE:(i + 1) * TILE] = block.T
    held[...] = contract(begin[...], gram[...], ((1,), (0,)))

    def iterate(step, carry):
        matrix = held[...]
        inner = contract(matrix, matrix, ((1,), (1,)))
        after = contract(matrix, gram[...], ((1,), (0,)))
        held[...] = contract(inverse_factor(inner, rows_ref), after, ((1,), (0,)))
        return carry

    lax.fori_loop(0, ITERS - 1, iterate, 0)
    matrix = held[...]
    inner = contract(matrix, matrix, ((1,), (1,)))
    after = contract(matrix, fib[...], ((1,), (0,)))
    inverse = inverse_factor(inner, rows_ref)
    basis[...] = contract(inverse, matrix, ((1,), (0,)))
    core[...] = contract(inverse, after, ((1,), (0,)))


def on_device(nf, ng, field, start):
    rows, columns = field.shape
    order, rank = start.shape
    width = columns // nf
    chunks = 4
    blocks = order // TILE
    unit = 8 * nf * ng
    units = -(-(blocks * (blocks + 1) // 2 * TILE) // unit)
    sizes = [n * unit for n in (units - units // 2, units // 2) if n]
    parts = [(sum(sizes[:p]), size) for p, size in enumerate(sizes)]
    packed_rows = sum(sizes)
    vmem = pl.BlockSpec(memory_space=pltpu.VMEM)
    f32 = jnp.float32
    dma = pltpu.SemaphoreType.DMA
    fib, packed, begin = pl.pallas_call(
        functools.partial(gram_kernel, nf, ng, chunks, parts, 1.0 / (columns * ng)),
        out_shape=(
            jax.ShapeDtypeStruct((order, width), f32),
            jax.ShapeDtypeStruct((packed_rows, TILE), f32),
            jax.ShapeDtypeStruct((rank, order), f32),
        ),
        in_specs=[pl.BlockSpec(memory_space=pltpu.HBM), vmem],
        out_specs=(vmem, vmem, vmem),
        scratch_shapes=[
            pltpu.VMEM((packed_rows, TILE), f32),
            pltpu.VMEM((2 * ng, packed_rows // 2 // ng, TILE), f32),
            pltpu.VMEM((nf // 2, packed_rows // nf // ng, TILE), f32),
            pltpu.VMEM((rank, 2 * rank), f32),
            dma((chunks,)),
            dma((chunks * nf,)), dma((chunks * nf,)),
            dma((8 * ng,)), dma((8 * ng,)),
            dma((2 * nf,)), dma((2 * nf,)),
        ],
        compiler_params=pltpu.CompilerParams(
            collective_id=0, has_side_effects=True, vmem_limit_bytes=50 * 2**20
        ),
        name="gram",
    )(field, start.T)
    basis, core = pl.pallas_call(
        basis_kernel,
        out_shape=(
            jax.ShapeDtypeStruct((rank, order), f32),
            jax.ShapeDtypeStruct((rank, width), f32),
        ),
        in_specs=[vmem] * 3,
        out_specs=(vmem, vmem),
        scratch_shapes=[
            pltpu.VMEM((order, order), f32),
            pltpu.VMEM((rank, order), f32),
            pltpu.VMEM((rank, 2 * rank), f32),
        ],
        compiler_params=pltpu.CompilerParams(vmem_limit_bytes=48 * 2**20),
        name="basis",
    )(packed, fib, begin)
    return basis.T, core


def solution(mesh):
    nf, ng = mesh.shape["fibre"], mesh.shape["group"]
    return jax.shard_map(
        functools.partial(on_device, nf, ng),
        mesh=mesh,
        in_specs=(P("fibre", "group"), P()),
        out_specs=(P(), P(None, ("group", "fibre"))),
        check_vma=False,
    )
```

```python
import functools

import jax
import jax.numpy as jnp
from jax import lax
from jax.experimental import pallas as pl
from jax.experimental.pallas import tpu as pltpu
from jax.sharding import PartitionSpec as P

ITERS = 3
TILE = 128
MESH = pl.DeviceIdType.MESH
HIGHEST = lax.Precision.HIGHEST


def contract(a, b, dims):
    return lax.dot_general(
        a, b, (dims, ((), ())), precision=HIGHEST, preferred_element_type=jnp.float32
    )


def aligned(start, size):
    return pl.ds(pl.multiple_of(start, 8), size)


def inverse_factor(a, rows_ref):
    n = a.shape[0]
    eye = (
        lax.broadcasted_iota(jnp.int32, (n, n), 0) == lax.broadcasted_iota(jnp.int32, (n, n), 1)
    ).astype(jnp.float32)
    w = jnp.concatenate([a, eye], axis=1)
    for k in range(0, n, 8):
        left = n - k
        cols = [jnp.broadcast_to(w[:, k + j:k + j + 1], (left, 2 * n)) for j in range(8)]
        for j in range(8):
            pivot = cols[j][j:j + 1, :]
            inv = lax.rsqrt(pivot)
            inv = inv * (1.5 - 0.5 * pivot * inv * inv)
            row = w[j:j + 1, :] * inv
            rows_ref[k + j:k + j + 1, :] = row
            below = cols[j] * inv
            w = w - below * row
            for m in range(j + 1, 8):
                cols[m] = cols[m] - below * (cols[m][j:j + 1, :] * inv)
        w = w[8:, :]
    return rows_ref[:, n:]


def block_places(blocks):
    places = {}
    for pair in reversed(range(0, blocks, 2)):
        for i in range(pair, min(pair + 2, blocks)):
            for j in range(i + 1):
                places[i, j] = len(places) * TILE
    return places


def orth(matrix, rows_ref):
    inverse = inverse_factor(contract(matrix, matrix, ((1,), (1,))), rows_ref)
    return contract(inverse, matrix, ((1,), (0,)))


def gram_kernel(
    nf, ng, chunks, parts, scale, field, start, fib, out, held,
    part, r1, r2, r3, rows_ref, own_sem,
    a_send, a_recv, c_send, c_recv, g_send, g_recv, z_send, z_recv,
):
    f = lax.axis_index("fibre")
    g = lax.axis_index("group")
    nz = nf // 2
    core = lax.rem(f, 2)
    z = f // 2
    mate = f + 1 - 2 * core
    rows, width = field.shape[0], fib.shape[1]
    order = fib.shape[0]
    span = width // chunks

    def remote(src, dst, send, recv, slot, device):
        copy = pltpu.make_async_remote_copy(
            src_ref=src, dst_ref=dst, send_sem=send.at[slot], recv_sem=recv.at[slot],
            device_id=device, device_id_type=MESH,
        )
        copy.start()
        return copy

    def fibre_peer(o):
        return lax.rem(f + o, nf)

    def group_device(o):
        return (f, lax.rem(g + o, ng))

    def z_device(o):
        return (lax.rem(z + o, nz) * 2 + core, g)

    barrier = pltpu.get_barrier_semaphore()
    for o in range(1, nf):
        pl.semaphore_signal(barrier, inc=1, device_id=(fibre_peer(o), g), device_id_type=MESH)
    for o in range(1, ng):
        pl.semaphore_signal(barrier, inc=1, device_id=group_device(o), device_id_type=MESH)
    pl.semaphore_wait(barrier, nf + ng - 2)

    far_first = sorted(range(1, nf), key=lambda o: abs(o - nf // 2))
    sends = []
    owns = []
    for c in range(chunks):
        here = fib.at[aligned(f * rows, rows), c * span:(c + 1) * span]
        sends.append([
            remote(
                field.at[:, pl.ds(pl.multiple_of(fibre_peer(o) * width + c * span, TILE), span)],
                here, a_send, a_recv, c * nf + o, (fibre_peer(o), g),
            )
            for o in far_first
        ])
        own = pltpu.make_async_copy(
            field.at[:, pl.ds(pl.multiple_of(f * width + c * span, TILE), span)], here, own_sem.at[c]
        )
        own.start()
        owns.append(own)

    held[...] = orth(start[...], rows_ref)

    def summed(p, first, size):
        half = size // 2
        quarter = half // ng
        piece = quarter // nz
        mine = first + core * half
        other = first + (1 - core) * half
        copy = remote(part.at[aligned(other, half), :], r1.at[0:half, :] if p == 0 else r1.at[r1.shape[0] - half:, :],
                      c_send, c_recv, 2 * p, (mate, g))
        yield
        copy.wait()
        base1 = 0 if p == 0 else r1.shape[0] - half
        part[aligned(mine, half), :] += r1[base1:base1 + half, :]

        at2 = 0 if p == 0 else r2.shape[1] - quarter
        copies = [
            remote(part.at[aligned(mine + lax.rem(g + o, ng) * quarter, quarter), :],
                   r2.at[o, at2:at2 + quarter, :], g_send, g_recv, 2 * p * ng + o, group_device(o))
            for o in range(1, ng)
        ]
        yield
        for copy in copies:
            copy.wait()
        mine = mine + g * quarter
        total = part[aligned(mine, quarter), :]
        for o in range(1, ng):
            total += r2[o, at2:at2 + quarter, :]
        part[aligned(mine, quarter), :] = total

        at3 = 0 if p == 0 else r3.shape[1] - piece
        copies = [
            remote(part.at[aligned(mine + lax.rem(z + o, nz) * piece, piece), :],
                   r3.at[o, at3:at3 + piece, :], z_send, z_recv, 2 * p * nz + o, z_device(o))
            for o in range(1, nz)
        ]
        yield
        for copy in copies:
            copy.wait()
        last = mine + z * piece
        total = part[aligned(last, piece), :]
        for o in range(1, nz):
            total += r3[o, at3:at3 + piece, :]
        out[aligned(last, piece), :] = total * scale

        block = out.at[aligned(last, piece), :]
        copies = [
            remote(block, block, z_send, z_recv, (2 * p + 1) * nz + o, z_device(o))
            for o in range(1, nz)
        ]
        yield
        for copy in copies:
            copy.wait()
        block = out.at[aligned(mine, quarter), :]
        copies = [
            remote(block, block, g_send, g_recv, (2 * p + 1) * ng + o, group_device(o))
            for o in range(1, ng)
        ]
        yield
        for copy in copies:
            copy.wait()
        block = out.at[aligned(first + core * half, half), :]
        copy = remote(block, block, c_send, c_recv, 2 * p + 1, (mate, g))
        yield
        copy.wait()

    blocks = order // TILE
    places = block_places(blocks)
    filled = len(places) * TILE
    if filled < part.shape[0]:
        part[filled:, :] = jnp.zeros((part.shape[0] - filled, TILE), jnp.float32)
    sums = []
    for c in range(chunks):
        for copy in sends[c]:
            copy.wait_recv()
        owns[c].wait()
        columns = slice(c * span, (c + 1) * span)
        done = 0
        for pair in reversed(range(0, blocks, 2)):
            top = min(pair + 2, blocks)
            strip = contract(fib[pair * TILE:top * TILE, columns], fib[:top * TILE, columns], ((1,), (1,)))
            for i in range(pair, top):
                for j in range(i + 1):
                    block = strip[(i - pair) * TILE:(i - pair + 1) * TILE, j * TILE:(j + 1) * TILE]
                    at = slice(places[i, j], places[i, j] + TILE)
                    part[at, :] = block if c == 0 else part[at, :] + block
                    done += TILE
            if c == chunks - 1:
                ready = part.shape[0] if done == filled else done
                while len(sums) < len(parts) and sum(parts[len(sums)]) <= ready:
                    step = summed(len(sums), *parts[len(sums)])
                    next(step)
                    sums.append(step)
    going = list(sums)
    while going:
        for step in list(going):
            try:
                next(step)
            except StopIteration:
                going.remove(step)

    for copies in sends:
        for copy in copies:
            copy.wait_send()


def basis_kernel(packed, fib, begin, basis, core, gram, held, rows_ref):
    for (i, j), at in block_places(fib.shape[0] // TILE).items():
        block = packed[at:at + TILE, :]
        gram[i * TILE:(i + 1) * TILE, j * TILE:(j + 1) * TILE] = block
        if j < i:
            gram[j * TILE:(j + 1) * TILE, i * TILE:(i + 1) * TILE] = block.T
    held[...] = contract(begin[...], gram[...], ((1,), (0,)))

    def iterate(step, carry):
        matrix = held[...]
        inner = contract(matrix, matrix, ((1,), (1,)))
        after = contract(matrix, gram[...], ((1,), (0,)))
        held[...] = contract(inverse_factor(inner, rows_ref), after, ((1,), (0,)))
        return carry

    lax.fori_loop(0, ITERS - 1, iterate, 0)
    matrix = held[...]
    inner = contract(matrix, matrix, ((1,), (1,)))
    after = contract(matrix, fib[...], ((1,), (0,)))
    inverse = inverse_factor(inner, rows_ref)
    basis[...] = contract(inverse, matrix, ((1,), (0,)))
    core[...] = contract(inverse, after, ((1,), (0,)))


def on_device(nf, ng, field, start):
    rows, columns = field.shape
    order, rank = start.shape
    width = columns // nf
    chunks = 2
    blocks = order // TILE
    unit = 8 * nf * ng
    units = -(-(blocks * (blocks + 1) // 2 * TILE) // unit)
    sizes = [n * unit for n in (units - units // 2, units // 2) if n]
    parts = [(sum(sizes[:p]), size) for p, size in enumerate(sizes)]
    packed_rows = sum(sizes)
    vmem = pl.BlockSpec(memory_space=pltpu.VMEM)
    f32 = jnp.float32
    dma = pltpu.SemaphoreType.DMA
    fib, packed, begin = pl.pallas_call(
        functools.partial(gram_kernel, nf, ng, chunks, parts, 1.0 / (columns * ng)),
        out_shape=(
            jax.ShapeDtypeStruct((order, width), f32),
            jax.ShapeDtypeStruct((packed_rows, TILE), f32),
            jax.ShapeDtypeStruct((rank, order), f32),
        ),
        in_specs=[pl.BlockSpec(memory_space=pltpu.HBM), vmem],
        out_specs=(vmem, vmem, vmem),
        scratch_shapes=[
            pltpu.VMEM((packed_rows, TILE), f32),
            pltpu.VMEM((packed_rows // 2, TILE), f32),
            pltpu.VMEM((ng, packed_rows // 2 // ng, TILE), f32),
            pltpu.VMEM((nf // 2, packed_rows // nf // ng, TILE), f32),
            pltpu.VMEM((rank, 2 * rank), f32),
            dma((chunks,)),
            dma((chunks * nf,)), dma((chunks * nf,)),
            dma((4,)), dma((4,)),
            dma((4 * ng,)), dma((4 * ng,)),
            dma((2 * nf,)), dma((2 * nf,)),
        ],
        compiler_params=pltpu.CompilerParams(
            collective_id=0, has_side_effects=True, vmem_limit_bytes=50 * 2**20
        ),
        name="gram",
    )(field, start.T)
    basis, core = pl.pallas_call(
        basis_kernel,
        out_shape=(
            jax.ShapeDtypeStruct((rank, order), f32),
            jax.ShapeDtypeStruct((rank, width), f32),
        ),
        in_specs=[vmem] * 3,
        out_specs=(vmem, vmem),
        scratch_shapes=[
            pltpu.VMEM((order, order), f32),
            pltpu.VMEM((rank, order), f32),
            pltpu.VMEM((rank, 2 * rank), f32),
        ],
        compiler_params=pltpu.CompilerParams(vmem_limit_bytes=48 * 2**20),
        name="basis",
    )(packed, fib, begin)
    return basis.T, core


def solution(mesh):
    nf, ng = mesh.shape["fibre"], mesh.shape["group"]
    return jax.shard_map(
        functools.partial(on_device, nf, ng),
        mesh=mesh,
        in_specs=(P("fibre", "group"), P()),
        out_specs=(P(), P(None, ("group", "fibre"))),
        check_vma=False,
    )
```
